128 devices in a mesh: dp: 32 (over x, y, core), vision: 4 (over z).
Axes of the slice: x: 4, y: 4, z: 4, core: 2. Of those that a mesh axis runs over, the one named last changes fastest.
Arguments:
- tokens: bfloat16 [16384, 3200], P(('dp', 'vision')), may hold values from -8 to 8
- gain: float32 [3200], replicated, may hold values from 0.1 to 1.9
- w_qkv: bfloat16 [3200, 6144], P(None, 'vision'), may hold values from -2 to 2
- w_out: bfloat16 [2048, 3200], P('vision'), may hold values from -0.125 to 0.125
- b_out: float32 [3200], replicated, may hold values from -3 to 3
- scale: float32 [3200], replicated, may hold values from 0.5 to 1.5
- dest: int32 [2048], replicated, may hold values from 0 to 2047, as said below
- d_owned: bfloat16 [16384, 3200], P(('dp', 'vision')), may hold values from -6 to 6
Outputs:
- y_owned: bfloat16 [16384, 3200], P(('dp', 'vision'))
- d_tokens: bfloat16 [16384, 3200], P(('dp', 'vision'))
- d_wqkv: bfloat16 [3200, 6144], P('dp', 'vision')
- d_wout: bfloat16 [2048, 3200], P('vision', 'dp')
- d_gain: float32 [3200], replicated
- d_scale: float32 [3200], replicated
- d_bias: float32 [3200], replicated
The draws below stay inside these ranges and needn't reach their ends.
Inputs may be any that keep to these rules, and one draw needn't show every extreme that they name: dest names a different slot for every block, so all 16 slots of every owner are filled (owner = slot // 16, a device index over dp and vision with dp slowest). Of the blocks of each device, exactly 16 / 4 go to owners of each vision index (owner % 4). The blocks of the devices of one index of dp fill at most 1 slots of any one owner.
All inputs are finite; a program needn't handle non-finite values.
Results may differ from the reference program's by a relative error of at most 0.025.
Values may be sent and summed in bfloat16 or wider, within the bound.
No kernel may reach another device: no remote copies, remote signals or barrier semaphores. Data moves between devices by JAX's collectives and lax.ppermute only.
A program may use at most 128 MiB of HBM per device.

```python
from functools import partial
import jax
import jax.numpy as jnp
from jax import lax

D = 3200
HEADS = 16
HEAD_DIM = 128
TILE = 256
SLOTS = 2
BLOCKS_DEV = 16
ROWS_DEV = 128
OWNER_SLOTS = 16
ROWS = 16384
BLOCKS = 2048
OWNER_ROWS = 16384
QKV = 6144
ATT = 2048
N_DP = 32
N_VISION = 4
DEVICES = 128


def draw_tokens(key, part):
    key = jax.random.fold_in(key, 3)
    values = jax.random.truncated_normal(key, -6.0, 6.0, (ROWS, D), jnp.float32)
    return values.astype(jnp.bfloat16)


def draw_w_qkv(key, part):
    key = jax.random.fold_in(key, 5)
    values = jax.random.truncated_normal(key, -4.0, 4.0, (D, QKV), jnp.float32) * D ** (-0.5)
    return values.astype(jnp.bfloat16)


def draw_dest(key, part):
    key = jax.random.fold_in(key, 7)
    owner_key, shift_key, member_key, local_key, slot_key = jax.random.split(key, 5)
    quota = BLOCKS_DEV // N_VISION
    total = N_VISION * N_DP * BLOCKS_DEV
    index = jnp.arange(total, dtype=jnp.int32)
    target_vision = index // (N_DP * BLOCKS_DEV)
    group = index // BLOCKS_DEV % N_DP
    step_index = index % BLOCKS_DEV
    owner_perm = jax.vmap(lambda sub: jax.random.permutation(sub, N_DP))(jax.random.split(owner_key, N_VISION)).astype(jnp.int32)
    group_shift = jax.vmap(lambda sub: jax.random.permutation(sub, N_DP))(jax.random.split(shift_key, N_VISION)).astype(jnp.int32)
    member_perm = jax.vmap(lambda sub: jax.random.permutation(sub, BLOCKS_DEV))(jax.random.split(member_key, N_VISION * N_DP)).astype(jnp.int32)
    local_perm = jax.vmap(lambda sub: jax.random.permutation(sub, BLOCKS_DEV))(jax.random.split(local_key, DEVICES)).astype(jnp.int32)
    slot_perm = jax.vmap(lambda sub: jax.random.permutation(sub, BLOCKS_DEV))(jax.random.split(slot_key, DEVICES)).astype(jnp.int32)
    owner_replica = owner_perm[target_vision, (group_shift[target_vision, group] + step_index) % N_DP]
    owner = owner_replica * N_VISION + target_vision
    member = member_perm[target_vision * N_DP + group, step_index]
    source_vision = member // quota
    within = member % quota
    device = group * N_VISION + source_vision
    local = local_perm[device, target_vision * quota + within]
    slot = slot_perm[owner, step_index]
    result = jnp.zeros((BLOCKS,), jnp.int32)
    result = result.at[device * BLOCKS_DEV + local].set(owner * OWNER_SLOTS + slot)
    return result


def shard_levels(key, dims, pieces, least, top_value):
    def one(dim, blocks):
        draws = jax.random.uniform(jax.random.fold_in(jax.random.fold_in(key, 6), dim), (blocks,), jnp.float32, least / len(pieces), top_value / len(pieces))
        return jnp.repeat(jnp.exp(draws), dims[dim] // blocks).reshape((-1,) + (1,) * (len(dims) - dim - 1))

    level = one(*pieces[0])
    for cut in pieces[1:]:
        level = level * one(*cut)
    return level


def noise(key, dims, scale, reach, cuts=(), kind=jnp.bfloat16):
    array = scale * jax.random.normal(key, dims, jnp.float32)
    if cuts:
        array = array * shard_levels(key, dims, cuts, -0.22, 0.18)
    return jnp.clip(array, -reach, reach).astype(kind)


def setup_inputs(seed: int = 0) -> dict:
    streams_of = jax.random.split(jax.random.key(seed), 9)
    tokens = draw_tokens(jax.random.fold_in(streams_of[8], 71), 0)
    gain = jnp.clip(1.0 + 0.18 * jax.random.normal(streams_of[1], (D,), jnp.float32), 0.1, 1.9)
    w_qkv = draw_w_qkv(jax.random.fold_in(streams_of[8], 71), 0)
    w_out = noise(streams_of[3], (ATT, D), ATT ** -0.5, 0.125, ((0, 4),))
    b_out = noise(streams_of[4], (D,), 0.5, 3.0, (), jnp.float32)
    scale = jnp.clip(jax.random.uniform(streams_of[5], (D,), jnp.float32, 0.5, 1.5), 0.5, 1.5)
    dest = draw_dest(jax.random.fold_in(streams_of[8], 71), 0)
    d_owned = noise(streams_of[7], (OWNER_ROWS, D), 1.0, 6.0, ((0, 128),))
    return {"tokens": tokens, "gain": gain, "w_qkv": w_qkv, "w_out": w_out, "b_out": b_out, "scale": scale, "dest": dest, "d_owned": d_owned}


EPSILON = 1e-06

def vision_sum(left, right):
    count = left.shape[0]
    inner = left.shape[1] // N_VISION
    left_parts = left.reshape(count, N_VISION, inner).astype(jnp.float32)
    right_parts = right.reshape(N_VISION, inner, right.shape[1]).astype(jnp.float32)
    partial_sums = jnp.einsum('rvk,vkd->vrd', left_parts, right_parts, precision=lax.Precision.HIGHEST)
    rounded = lax.optimization_barrier(partial_sums.astype(jnp.bfloat16))
    return lax.optimization_barrier(jnp.sum(rounded.astype(jnp.float32), axis=0))

def replica_pass(carry, inputs, gain, w_qkv, w_out, b_out, scale):
    token_rows, d_output = inputs
    replica_rows = token_rows.shape[0]
    tiles = replica_rows // TILE
    factor = HEAD_DIM ** (-0.5)
    token_f = token_rows.astype(jnp.float32)
    inverse = lax.rsqrt(lax.optimization_barrier(jnp.mean(token_f * token_f, axis=-1, keepdims=True)) + EPSILON)
    normed = (token_f * inverse * gain).astype(jnp.bfloat16)
    qkv = jnp.dot(normed, w_qkv, preferred_element_type=jnp.float32).astype(jnp.bfloat16)
    parts = qkv.reshape(tiles, TILE, HEADS, 3, HEAD_DIM).astype(jnp.float32)
    query = parts[:, :, :, 0]
    key_rows = parts[:, :, :, 1]
    value_rows = parts[:, :, :, 2]
    highest = lax.Precision.HIGHEST
    scores = jnp.einsum('tqhd,tkhd->thqk', query, key_rows, precision=highest) * factor
    probs = jax.nn.softmax(scores, axis=-1)
    probs_b = probs.astype(jnp.bfloat16).astype(jnp.float32)
    attended = jnp.einsum('thqk,tkhd->tqhd', probs_b, value_rows, precision=highest).astype(jnp.bfloat16)
    attended = attended.reshape(replica_rows, HEADS * HEAD_DIM)
    projected = vision_sum(attended, w_out) + b_out
    output = (token_f + scale * projected).astype(jnp.bfloat16)
    d_out_f = d_output.astype(jnp.float32)
    scale_part = lax.optimization_barrier(jnp.sum(d_out_f * projected, axis=0))
    bias_part = lax.optimization_barrier(jnp.sum(d_out_f * scale, axis=0))
    d_projected = (d_out_f * scale).astype(jnp.bfloat16)
    d_attended = jnp.dot(d_projected, w_out.T, preferred_element_type=jnp.float32).astype(jnp.bfloat16)
    out_part = lax.optimization_barrier(jnp.dot(attended.T, d_projected, preferred_element_type=jnp.float32).astype(jnp.bfloat16))
    d_att = d_attended.reshape(tiles, TILE, HEADS, HEAD_DIM).astype(jnp.float32)
    d_probs = jnp.einsum('tqhd,tkhd->thqk', d_att, value_rows, precision=highest)
    d_values = jnp.einsum('thqk,tqhd->tkhd', probs_b, d_att, precision=highest).astype(jnp.bfloat16)
    d_scores = (probs * (d_probs - lax.optimization_barrier(jnp.sum(probs * d_probs, axis=-1, keepdims=True))) * factor).astype(jnp.bfloat16)
    d_scores_f = d_scores.astype(jnp.float32)
    d_query = jnp.einsum('thqk,tkhd->tqhd', d_scores_f, key_rows, precision=highest).astype(jnp.bfloat16)
    d_keys = jnp.einsum('thqk,tqhd->tkhd', d_scores_f, query, precision=highest).astype(jnp.bfloat16)
    d_qkv = jnp.stack([d_query, d_keys, d_values], axis=3).reshape(replica_rows, QKV)
    qkv_part = lax.optimization_barrier(jnp.dot(normed.T, d_qkv, preferred_element_type=jnp.float32).astype(jnp.bfloat16))
    d_normed = vision_sum(d_qkv, w_qkv.T)
    scaled = d_normed * gain
    gain_part = lax.optimization_barrier(jnp.sum(d_normed * token_f * inverse, axis=0))
    d_tokens = d_out_f + inverse * scaled - token_f * inverse ** 3 * lax.optimization_barrier(jnp.mean(scaled * token_f, axis=-1, keepdims=True))
    carry = (carry[0] + qkv_part.astype(jnp.float32), carry[1] + out_part.astype(jnp.float32), carry[2] + gain_part, carry[3] + scale_part, carry[4] + bias_part)
    return (carry, (output, d_tokens.astype(jnp.bfloat16)))

def reference(tokens, gain, w_qkv, w_out, b_out, scale, dest, d_owned):
    width = tokens.shape[1]
    block_rows = ROWS_DEV // BLOCKS_DEV
    owner_blocks = d_owned.reshape(DEVICES * OWNER_SLOTS, block_rows, width)
    d_output = owner_blocks[dest].reshape(ROWS, width)
    replica_rows = SLOTS * TILE
    token_groups = tokens.reshape(N_DP, replica_rows, width)
    d_groups = d_output.reshape(N_DP, replica_rows, width)
    initial = (jnp.zeros((width, QKV), jnp.float32), jnp.zeros((ATT, width), jnp.float32), jnp.zeros((width,), jnp.float32), jnp.zeros((width,), jnp.float32), jnp.zeros((width,), jnp.float32))
    advance = partial(replica_pass, gain=gain, w_qkv=w_qkv, w_out=w_out, b_out=b_out, scale=scale)
    carry, (outputs, d_tokens) = lax.scan(advance, initial, (token_groups, d_groups))
    output_blocks = outputs.reshape(ROWS // block_rows, block_rows, width)
    owned = jnp.zeros((DEVICES * OWNER_SLOTS, block_rows, width), jnp.bfloat16).at[dest].set(output_blocks)
    return (owned.reshape(OWNER_ROWS, width), d_tokens.reshape(ROWS, width), carry[0].astype(jnp.bfloat16), carry[1].astype(jnp.bfloat16), carry[2], carry[3], carry[4])
```

```python
import functools

import jax
import jax.numpy as jnp
from jax import lax
from jax.experimental import pallas as pl
from jax.experimental.pallas import tpu as pltpu
from jax.sharding import PartitionSpec as P

HEAD_DIM = 128
TILE = 256
BLOCK = 8
EPSILON = 1e-06
bf16 = jnp.bfloat16
f32 = jnp.float32


def cast(x, dtype):
    return x.astype(dtype)


def gather_body(count, index_ref, source_ref, out_ref, sems):
    for i in range(count):
        pltpu.make_async_copy(source_ref.at[index_ref[i]], out_ref.at[i], sems.at[i]).start()
    for i in range(count):
        pltpu.make_async_copy(source_ref.at[index_ref[i]], out_ref.at[i], sems.at[i]).wait()


def gather_blocks(index, source):
    count = index.shape[0]
    return pl.pallas_call(
        functools.partial(gather_body, count),
        out_shape=jax.ShapeDtypeStruct((count,) + source.shape[1:], source.dtype),
        in_specs=[
            pl.BlockSpec(memory_space=pltpu.SMEM),
            pl.BlockSpec(memory_space=pl.ANY),
        ],
        out_specs=pl.BlockSpec(memory_space=pl.ANY),
        scratch_shapes=[pltpu.SemaphoreType.DMA((count,))],
    )(index, source)


def softmax_of(query, keys, factor):
    scores = (
        lax.dot_general(query, keys, (((1,), (1,)), ((), ())), preferred_element_type=f32) * factor
    )
    top = jnp.max(scores, axis=-1, keepdims=True)
    weights = jnp.exp(scores - top)
    return weights / jnp.sum(weights, axis=-1, keepdims=True)


def permutation(place_ref, rows):
    columns = lax.broadcasted_iota(jnp.int32, (rows, rows), 1)
    return (place_ref[...] == columns).astype(f32).astype(bf16)


def attend_body(factor, heads, qkv_ref, place_ref, out_ref, held):
    rows = qkv_ref.shape[0]
    for h in range(heads):
        for t in range(rows // TILE):
            span = slice(t * TILE, (t + 1) * TILE)
            at = 3 * h * HEAD_DIM
            query = qkv_ref[span, at : at + HEAD_DIM]
            keys = qkv_ref[span, at + HEAD_DIM : at + 2 * HEAD_DIM]
            values = qkv_ref[span, at + 2 * HEAD_DIM : at + 3 * HEAD_DIM]
            probs = softmax_of(query, keys, factor).astype(bf16)
            held[span, h * HEAD_DIM : (h + 1) * HEAD_DIM] = jnp.dot(
                probs, values, preferred_element_type=f32
            ).astype(bf16)
    perm = permutation(place_ref, rows)
    out_ref[...] = lax.dot_general(
        perm, held[...], (((0,), (0,)), ((), ())), preferred_element_type=f32
    ).astype(bf16)


def attend(qkv, place):
    rows, columns = qkv.shape
    heads = columns // (3 * HEAD_DIM)
    return pl.pallas_call(
        functools.partial(attend_body, HEAD_DIM**-0.5, heads),
        out_shape=jax.ShapeDtypeStruct((rows, heads * HEAD_DIM), bf16),
        scratch_shapes=[pltpu.VMEM((rows, heads * HEAD_DIM), bf16)],
        compiler_params=pltpu.CompilerParams(vmem_limit_bytes=32 * 2**20),
    )(qkv, place)


def attend_back_body(factor, heads, qkv_ref, d_ref, place_ref, out_ref, held):
    rows = qkv_ref.shape[0]
    perm = permutation(place_ref, rows)
    held[...] = jnp.dot(perm, d_ref[...], preferred_element_type=f32).astype(bf16)
    for h in range(heads):
        for t in range(rows // TILE):
            span = slice(t * TILE, (t + 1) * TILE)
            at = 3 * h * HEAD_DIM
            query = qkv_ref[span, at : at + HEAD_DIM]
            keys = qkv_ref[span, at + HEAD_DIM : at + 2 * HEAD_DIM]
            values = qkv_ref[span, at + 2 * HEAD_DIM : at + 3 * HEAD_DIM]
            d_att = held[span, h * HEAD_DIM : (h + 1) * HEAD_DIM]
            probs = softmax_of(query, keys, factor)
            d_probs = lax.dot_general(
                d_att, values, (((1,), (1,)), ((), ())), preferred_element_type=f32
            )
            d_values = lax.dot_general(
                probs.astype(bf16), d_att, (((0,), (0,)), ((), ())), preferred_element_type=f32
            )
            inner = jnp.sum(probs * d_probs, axis=-1, keepdims=True)
            d_scores = (probs * (d_probs - inner) * factor).astype(bf16)
            d_query = jnp.dot(d_scores, keys, preferred_element_type=f32)
            d_keys = lax.dot_general(
                d_scores, query, (((0,), (0,)), ((), ())), preferred_element_type=f32
            )
            out_ref[span, at : at + HEAD_DIM] = d_query.astype(bf16)
            out_ref[span, at + HEAD_DIM : at + 2 * HEAD_DIM] = d_keys.astype(bf16)
            out_ref[span, at + 2 * HEAD_DIM : at + 3 * HEAD_DIM] = d_values.astype(bf16)


def attend_back(qkv, d_attended, place):
    rows, columns = qkv.shape
    heads = columns // (3 * HEAD_DIM)
    return pl.pallas_call(
        functools.partial(attend_back_body, HEAD_DIM**-0.5, heads),
        out_shape=jax.ShapeDtypeStruct((rows, columns), bf16),
        scratch_shapes=[pltpu.VMEM((rows, heads * HEAD_DIM), bf16)],
        compiler_params=pltpu.CompilerParams(vmem_limit_bytes=32 * 2**20),
    )(qkv, d_attended, place)


def swap_vision(x, flip):
    return lax.ppermute(x, "vision", [(i, i ^ flip) for i in range(4)])


def swap_dp(x, flip):
    return lax.ppermute(x, "dp", [(i, i ^ flip) for i in range(32)])


def gather_ring(x, swap):
    half = x.shape[0] // 2
    one = swap(x, 1)
    three = swap(x, 3)
    two_low = swap(one[:half], 3)
    two_high = swap(three[half:], 1)
    return [x, one, two_low, two_high, three]


def scatter_ring(parts, swap):
    own, one, two, three = parts
    half = two.shape[0] // 2
    low = swap(two[:half], 1)
    high = swap(two[half:], 3)
    three = jnp.concatenate([(three[:half].astype(f32) + low.astype(f32)).astype(bf16), three[half:]])
    one = jnp.concatenate([one[:half], (one[half:].astype(f32) + high.astype(f32)).astype(bf16)])
    from_one = swap(one, 1)
    from_three = swap(three, 3)
    return own.astype(f32) + from_one.astype(f32) + from_three.astype(f32)


def sum_everywhere(x):
    for flip in (1, 2, 6, 8, 24):
        x = x + swap_dp(x, flip)
    for flip in (1, 3):
        x = x + swap_vision(x, flip)
    return x


def swap_x(x, flip):
    return swap_dp(x, flip * 8)


def swap_y(x, flip):
    return swap_dp(x, flip * 2)


def pick(x, index, axis=0):
    return lax.dynamic_index_in_dim(x, index, axis, keepdims=False)


def replica_sum(wide, replica_rank):
    x_rank, y_rank, core = replica_rank // 8, replica_rank // 2 % 4, replica_rank % 2
    width = wide[0].shape[0]
    chip_rows = width // 16

    def half(index):
        return jnp.concatenate(
            [lax.dynamic_slice_in_dim(w, index * (w.shape[1] // 2), w.shape[1] // 2, 1) for w in wide],
            axis=1,
        )

    away = swap_dp(half(1 - core), 1)
    total = (half(core).astype(f32) + away.astype(f32)).astype(bf16)
    columns = total.shape[1] // 2
    left = total[:, :columns].reshape(4, 4 * chip_rows, columns)
    right = total[:, columns:].reshape(4, 4, chip_rows, columns)
    left = scatter_ring([pick(left, x_rank ^ j) for j in range(4)], swap_x).astype(bf16)
    right = scatter_ring([pick(right, y_rank ^ j, 1) for j in range(4)], swap_y).astype(bf16)
    left = left.reshape(4, chip_rows, columns)
    left = scatter_ring([pick(left, y_rank ^ j) for j in range(4)], swap_y)
    right = scatter_ring([pick(right, x_rank ^ j) for j in range(4)], swap_x)
    both = jnp.concatenate([left, right], axis=1).astype(bf16)
    rows = chip_rows // 2
    here = lax.dynamic_slice_in_dim(both, core * rows, rows, 0)
    there = swap_dp(lax.dynamic_slice_in_dim(both, (1 - core) * rows, rows, 0), 1)
    low = jnp.where(core == 0, here, there)
    high = jnp.where(core == 0, there, here)
    outs, at = [], 0
    for w in wide:
        n = w.shape[1] // 2
        outs.append(jnp.concatenate([low[:, at : at + n], high[:, at : at + n]], axis=1))
        at += n
    return outs


def tables(dest, replica_rank, vision_rank):
    everyone = dest.reshape(32, 64)
    me = replica_rank * 4 + vision_rank
    row = lax.dynamic_index_in_dim(everyone, replica_rank, 0, keepdims=False)
    owner_vision = row // 16 % 4
    owner_replica = row // 64
    j = jnp.arange(64, dtype=jnp.int32)
    source = j // 16
    same = (
        (owner_vision[:, None] == owner_vision[None])
        & (source[:, None] == source[None])
        & (j[None] < j[:, None])
    )
    rank = jnp.sum(same.astype(jnp.int32), axis=1)
    arrival = (owner_vision ^ vision_rank) * 16 + (source ^ owner_vision) * 4 + rank
    order = (source ^ vision_rank) * 16 + j % 16

    def table(at, values, count):
        hit = at[None] == jnp.arange(count, dtype=jnp.int32)[:, None]
        return jnp.sum(jnp.where(hit, values[None], 0), axis=1)

    arrival_of_row = table(order, arrival, 64)
    row_of_arrival = table(arrival, order, 16)
    replica_of_held = table(arrival, owner_replica, 16)
    held_of_replica = table(replica_of_held, jnp.arange(16, dtype=jnp.int32), 32)
    slot_of_replica = jnp.sum(jnp.where(everyone // 16 == me, everyone % 16, 0), axis=1)
    hit = everyone[None] == (me * 16 + jnp.arange(16, dtype=jnp.int32))[:, None, None]
    replica_of_slot = jnp.sum(
        jnp.where(hit, jnp.arange(32, dtype=jnp.int32)[None, :, None], 0), axis=(1, 2)
    )
    return (
        arrival_of_row,
        row_of_arrival,
        replica_of_held,
        held_of_replica,
        slot_of_replica,
        replica_of_slot,
    )


def body(tokens, gain, w_qkv, w_out, b_out, scale, dest, d_owned):
    vision_rank = lax.axis_index("vision")
    replica_rank = lax.axis_index("dp")
    rows_dev, width = tokens.shape
    blocks_dev = rows_dev // BLOCK

    def blocks(x):
        return x.reshape(-1, BLOCK, width)

    def to_dp(x):
        return lax.all_to_all(x, "dp", split_axis=0, concat_axis=0, tiled=True)

    (
        arrival_of_row,
        row_of_arrival,
        replica_of_held,
        held_of_replica,
        slot_of_replica,
        replica_of_slot,
    ) = tables(dest, replica_rank, vision_rank)
    place = (arrival_of_row[:, None] * BLOCK + jnp.arange(BLOCK, dtype=jnp.int32)[None]).reshape(-1, 1)

    token_parts = gather_ring(tokens, swap_vision)
    back = to_dp(gather_blocks(slot_of_replica, blocks(d_owned)))
    d_held = gather_blocks(replica_of_held, back).reshape(rows_dev, width)
    d_parts = gather_ring(d_held, swap_vision)

    token_rows = jnp.concatenate(token_parts)
    token_f = token_rows.astype(f32)
    inverse = lax.rsqrt(jnp.mean(token_f * token_f, axis=-1, keepdims=True) + EPSILON)
    normed = (token_f * inverse * gain).astype(bf16)
    qkv = jnp.dot(normed, w_qkv, preferred_element_type=f32).astype(bf16)
    attended = attend(qkv, place)

    head_parts = jnp.dot(attended, w_out, preferred_element_type=f32).astype(bf16)
    chunks = [head_parts[i * rows_dev : (i + 1) * rows_dev] for i in range(4)]
    projected = scatter_ring(chunks, swap_vision) + b_out
    held_tokens = gather_blocks(row_of_arrival, blocks(token_rows)).reshape(rows_dev, width)
    output = (held_tokens.astype(f32) + scale * projected).astype(bf16)
    d_held_f = d_held.astype(f32)
    local_scale = jnp.sum(d_held_f * projected, axis=0)
    local_bias = jnp.sum(d_held_f * scale, axis=0)
    arrived = to_dp(gather_blocks(held_of_replica, blocks(output)))
    y_owned = gather_blocks(replica_of_slot, arrived).reshape(rows_dev, width)

    d_rows = jnp.concatenate(d_parts)
    d_projected = (d_rows.astype(f32) * scale).astype(bf16)
    d_attended = lax.dot_general(
        d_projected, w_out, (((1,), (1,)), ((), ())), preferred_element_type=f32
    ).astype(bf16)
    d_qkv = attend_back(qkv, d_attended, place)
    normed_full = lax.dot_general(
        d_qkv, w_qkv, (((1,), (1,)), ((), ())), preferred_element_type=f32
    )
    local_gain = jnp.sum(normed_full * (token_f * inverse), axis=0)
    normed_parts = normed_full.astype(bf16)
    chunks = [normed_parts[i * rows_dev : (i + 1) * rows_dev] for i in range(4)]
    d_normed = scatter_ring(chunks, swap_vision)

    wout_part = lax.dot_general(
        d_projected, attended, (((0,), (0,)), ((), ())), preferred_element_type=f32
    ).astype(bf16)
    wqkv_part = lax.dot_general(
        normed, d_qkv, (((0,), (0,)), ((), ())), preferred_element_type=f32
    ).astype(bf16)
    d_wqkv, d_wout = replica_sum([wqkv_part, wout_part], replica_rank)

    sums = sum_everywhere(jnp.stack([local_gain, local_scale, local_bias]))

    own_f = tokens.astype(f32)
    own_inverse = inverse[:rows_dev]
    d_output = gather_blocks(arrival_of_row[:blocks_dev], blocks(d_rows)).reshape(rows_dev, width)
    scaled = d_normed * gain
    d_tokens = (
        d_output.astype(f32)
        + own_inverse * scaled
        - own_f * own_inverse**3 * jnp.mean(scaled * own_f, axis=-1, keepdims=True)
    ).astype(bf16)
    return y_owned, d_tokens, d_wqkv, d_wout.T, sums[0], sums[1], sums[2]


def solution(mesh):
    placed = (
        P(("dp", "vision"), None),
        P(),
        P(None, "vision"),
        P("vision", None),
        P(),
        P(),
        P(),
        P(("dp", "vision"), None),
    )
    return jax.shard_map(
        body,
        mesh=mesh,
        in_specs=placed,
        out_specs=(
            P(("dp", "vision"), None),
            P(("dp", "vision"), None),
            P("dp", "vision"),
            P("vision", "dp"),
            P(),
            P(),
            P(),
        ),
        check_vma=False,
    )
```

```python
import functools

import jax
import jax.numpy as jnp
from jax import lax
from jax.experimental import pallas as pl
from jax.experimental.pallas import tpu as pltpu
from jax.sharding import PartitionSpec as P

HEAD_DIM = 128
TILE = 256
BLOCK = 8
EPSILON = 1e-06
bf16 = jnp.bfloat16
f32 = jnp.float32


INDEX = pl.BlockSpec(memory_space=pltpu.SMEM)
LOCAL = pl.BlockSpec(memory_space=pltpu.VMEM)
PLACED = pl.BlockSpec(memory_space=pl.ANY)


def call(kernel, outs, index=(), local=(), fetched=(), scratch=(), after=(), mib=28, flops=0):
    first, second, third = len(index), len(local), len(fetched)

    def body(*refs):
        at = first + second
        sources = refs[at : at + third]
        at += third + len(after)
        results = refs[at : at + len(outs)]
        at += len(outs)
        buffers = refs[at : at + third]
        at += third
        copies = []
        if third:
            sems = refs[at]
            at += 1
            for n, (source, buffer) in enumerate(zip(sources, buffers)):
                copies.append(pltpu.make_async_copy(source, buffer, sems.at[n]))
                copies[-1].start()
        given = list(refs[: first + second]) + list(buffers)
        if third:
            kernel(copies, *given, *results, *refs[at:])
        else:
            kernel(*given, *results, *refs[at:])

    scratch_shapes = [pltpu.VMEM(x.shape, x.dtype) for x in fetched]
    if third:
        scratch_shapes.append(pltpu.SemaphoreType.DMA((third,)))
    result = pl.pallas_call(
        body,
        out_shape=tuple(jax.ShapeDtypeStruct(*o) for o in outs),
        in_specs=[INDEX] * first + [LOCAL] * second + [PLACED] * (third + len(after)),
        out_specs=tuple([LOCAL] * len(outs)),
        scratch_shapes=scratch_shapes + list(scratch),
        compiler_params=pltpu.CompilerParams(vmem_limit_bytes=mib * 2**20),
        cost_estimate=pl.CostEstimate(flops=flops, bytes_accessed=1 << 20, transcendentals=0),
    )(*index, *local, *fetched, *after)
    return result if len(outs) > 1 else result[0]


def gather_body(index_ref, source_ref, out_ref):
    for i in range(out_ref.shape[0]):
        out_ref[i] = source_ref[index_ref[i]]


def gather_blocks(index, source):
    shape = (index.shape[0],) + source.shape[1:]
    return call(gather_body, [(shape, source.dtype)], [index], [source], mib=16)


def ring_total(own_ref, ring_refs, i):
    one_low, one_high, three_low, three_high = ring_refs
    half = one_low.shape[0]
    one = one_low[i] if i < half else one_high[i - half]
    three = three_low[i] if i < half else three_high[i - half]
    return own_ref[i].astype(f32) + one.astype(f32) + three.astype(f32)


def output_body(
    copies, row_ref, send_ref, token_ref, bias_ref, scale_ref, held_ref, own_ref, r1, r2, r3, r4,
    out_ref, sums_ref, made, by_scale, by_bias,
):
    scale = scale_ref[...]
    bias = bias_ref[...]
    for copy in copies:
        copy.wait()
    for i in range(own_ref.shape[0]):
        projected = ring_total(own_ref, (r1, r2, r3, r4), i) + bias
        tokens = token_ref[row_ref[i]].astype(f32)
        made[i] = (tokens + scale * projected).astype(bf16)
        d_output = held_ref[i].astype(f32)
        if i == 0:
            by_scale[...] = d_output * projected
            by_bias[...] = d_output * scale
        else:
            by_scale[...] += d_output * projected
            by_bias[...] += d_output * scale
    sums_ref[0:1] = jnp.sum(by_scale[...], axis=0, keepdims=True)
    sums_ref[1:2] = jnp.sum(by_bias[...], axis=0, keepdims=True)
    for i in range(out_ref.shape[0]):
        out_ref[i] = made[send_ref[i]]


def make_output(rows, sends, tokens, held, own, ring, bias, scale, after):
    count, _, width = own.shape
    return call(
        output_body,
        [((sends.shape[0], BLOCK, width), bf16), ((2, width), f32)],
        [rows, sends],
        [tokens, bias, scale],
        [held, own, *ring],
        [
            pltpu.VMEM((count, BLOCK, width), bf16),
            pltpu.VMEM((BLOCK, width), f32),
            pltpu.VMEM((BLOCK, width), f32),
        ],
        after,
        mib=20,
    )


def d_tokens_body(copies, row_ref, gain_ref, token_ref, d_ref, own_ref, r1, r2, r3, r4, out_ref):
    gain = gain_ref[...]
    for copy in copies:
        copy.wait()
    for i in range(own_ref.shape[0]):
        tokens = token_ref[i].astype(f32)
        inverse = lax.rsqrt(jnp.mean(tokens * tokens, axis=-1, keepdims=True) + EPSILON)
        scaled = ring_total(own_ref, (r1, r2, r3, r4), i) * gain
        inner = jnp.mean(scaled * tokens, axis=-1, keepdims=True)
        d_output = d_ref[row_ref[i]].astype(f32)
        out_ref[i] = (
            d_output + inverse * scaled - tokens * (inverse * inverse * inverse * inner)
        ).astype(bf16)


def make_d_tokens(rows, tokens, d_rows, own, ring, gain):
    return call(
        d_tokens_body, [(tokens.shape, bf16)], [rows], [gain], [tokens, d_rows, own, *ring], mib=16
    )


def norm_rows(token_ref, gain, normed_ref, inverse_ref, start):
    rows = 32

    def some(k, _):
        tokens = token_ref[pl.ds(pl.multiple_of(k * rows, rows), rows), :].astype(f32)
        inverse = lax.rsqrt(jnp.mean(tokens * tokens, axis=-1, keepdims=True) + EPSILON)
        to = pl.ds(pl.multiple_of(start + k * rows, rows), rows)
        inverse_ref[to, :] = inverse
        normed_ref[to, :] = (tokens * inverse * gain).astype(bf16)
        return 0

    lax.fori_loop(0, token_ref.shape[0] // rows, some, 0)


def norm_body(count, *refs):
    gain = refs[count][...]
    start = 0
    for ref in refs[:count]:
        norm_rows(ref, gain, refs[count + 1], refs[count + 2], start)
        start += ref.shape[0]


def norm(parts, gain):
    rows = sum(p.shape[0] for p in parts)
    return call(
        functools.partial(norm_body, len(parts)),
        [((rows, gain.shape[1]), bf16), ((rows, 1), f32)],
        local=[*parts, gain],
        mib=12,
    )


def softmax_of(query, keys, factor):
    scores = (
        lax.dot_general(query, keys, (((1,), (1,)), ((), ())), preferred_element_type=f32) * factor
    )
    top = jnp.max(scores, axis=-1, keepdims=True)
    weights = jnp.exp(scores - top)
    return weights / jnp.sum(weights, axis=-1, keepdims=True)


def permutation(place_ref, rows):
    columns = lax.broadcasted_iota(jnp.int32, (rows, rows), 1)
    return (place_ref[...] == columns).astype(f32).astype(bf16)


def forward_body(
    factor, n0, i0, n13, i13, t2, t3, gain_ref, place_ref, w_ref,
    normed_ref, inverse_ref, qkv_ref, attended_ref, held,
):
    rows = normed_ref.shape[0]
    part = rows // 4
    normed_ref[:part] = n0[...]
    normed_ref[part : 2 * part] = n13[:part]
    normed_ref[3 * part :] = n13[part:]
    inverse_ref[:part] = i0[...]
    inverse_ref[part : 2 * part] = i13[:part]
    inverse_ref[3 * part :] = i13[part:]
    norm_rows(t2, gain_ref[...], normed_ref, inverse_ref, 2 * part)
    norm_rows(t3, gain_ref[...], normed_ref, inverse_ref, 2 * part + part // 2)
    for n in range(qkv_ref.shape[1] // 256):
        span = slice(n * 256, (n + 1) * 256)
        qkv_ref[:, span] = jnp.dot(
            normed_ref[...], w_ref[:, span], preferred_element_type=f32
        ).astype(bf16)
    for h in range(qkv_ref.shape[1] // (3 * HEAD_DIM)):
        for t in range(rows // TILE):
            span = slice(t * TILE, (t + 1) * TILE)
            at = 3 * h * HEAD_DIM
            query = qkv_ref[span, at : at + HEAD_DIM]
            keys = qkv_ref[span, at + HEAD_DIM : at + 2 * HEAD_DIM]
            values = qkv_ref[span, at + 2 * HEAD_DIM : at + 3 * HEAD_DIM]
            probs = softmax_of(query, keys, factor).astype(bf16)
            held[span, h * HEAD_DIM : (h + 1) * HEAD_DIM] = jnp.dot(
                probs, values, preferred_element_type=f32
            ).astype(bf16)
    perm = permutation(place_ref, rows)
    attended_ref[...] = lax.dot_general(
        perm, held[...], (((0,), (0,)), ((), ())), preferred_element_type=f32
    ).astype(bf16)


def forward(own, neighbours, opposite, gain, place, w_qkv, after):
    width, columns = w_qkv.shape
    rows = place.shape[0]
    return call(
        functools.partial(forward_body, HEAD_DIM**-0.5),
        [
            ((rows, width), bf16),
            ((rows, 1), f32),
            ((rows, columns), bf16),
            ((rows, columns // 3), bf16),
        ],
        local=[*own, *neighbours, *opposite, gain, place, w_qkv],
        scratch=[pltpu.VMEM((rows, columns // 3), bf16)],
        after=after,
        mib=32,
        flops=2 * rows * width * columns,
    )


def split_rows(value, refs, span):
    at = 0
    for ref in refs:
        ref[:, span] = value[at : at + ref.shape[0]].astype(ref.dtype)
        at += ref.shape[0]


PIECES = (128, 64, 64, 64, 64, 64, 64)
STEP = 640


def head_body(attended_ref, w_ref, *out_refs):
    for at in range(0, w_ref.shape[1], STEP):
        span = slice(at, at + STEP)
        full = jnp.dot(attended_ref[...], w_ref[:, span], preferred_element_type=f32)
        split_rows(full, out_refs, span)


def project(attended, w_out, after):
    rows, depth = attended.shape
    width = w_out.shape[1]
    return call(
        head_body,
        [((n, width), bf16) for n in PIECES],
        local=[attended, w_out],
        after=after,
        flops=2 * rows * width * depth,
    )


def back_body(
    factor, copies, scale_ref, w_ref, qkv_ref, place_ref, d0, d1, d2, d3, d4,
    scaled_ref, out_ref, held,
):
    rows = qkv_ref.shape[0]
    at = 0
    for copy, ref in zip(copies, (d0, d1, d2, d3, d4)):
        copy.wait()
        scaled_ref[at : at + ref.shape[0]] = (ref[...].astype(f32) * scale_ref[...]).astype(bf16)
        at += ref.shape[0]
    total = lax.dot_general(
        scaled_ref[...], w_ref[...], (((1,), (1,)), ((), ())), preferred_element_type=f32
    ).astype(bf16)
    perm = permutation(place_ref, rows)
    held[...] = jnp.dot(perm, total, preferred_element_type=f32).astype(bf16)
    for h in range(qkv_ref.shape[1] // (3 * HEAD_DIM)):
        for t in range(rows // TILE):
            span = slice(t * TILE, (t + 1) * TILE)
            at = 3 * h * HEAD_DIM
            query = qkv_ref[span, at : at + HEAD_DIM]
            keys = qkv_ref[span, at + HEAD_DIM : at + 2 * HEAD_DIM]
            values = qkv_ref[span, at + 2 * HEAD_DIM : at + 3 * HEAD_DIM]
            d_att = held[span, h * HEAD_DIM : (h + 1) * HEAD_DIM]
            probs = softmax_of(query, keys, factor)
            d_probs = lax.dot_general(
                d_att, values, (((1,), (1,)), ((), ())), preferred_element_type=f32
            )
            d_values = lax.dot_general(
                probs.astype(bf16), d_att, (((0,), (0,)), ((), ())), preferred_element_type=f32
            )
            inner = jnp.sum(probs * d_probs, axis=-1, keepdims=True)
            d_scores = (probs * (d_probs - inner) * factor).astype(bf16)
            d_query = jnp.dot(d_scores, keys, preferred_element_type=f32)
            d_keys = lax.dot_general(
                d_scores, query, (((0,), (0,)), ((), ())), preferred_element_type=f32
            )
            out_ref[span, at : at + HEAD_DIM] = d_query.astype(bf16)
            out_ref[span, at + HEAD_DIM : at + 2 * HEAD_DIM] = d_keys.astype(bf16)
            out_ref[span, at + 2 * HEAD_DIM : at + 3 * HEAD_DIM] = d_values.astype(bf16)


def backward(parts, scale, w_out, qkv, place, after):
    depth, width = w_out.shape
    rows, columns = qkv.shape
    return call(
        functools.partial(back_body, HEAD_DIM**-0.5),
        [((rows, width), bf16), ((rows, columns), bf16)],
        local=[scale, w_out, qkv, place],
        fetched=parts,
        scratch=[pltpu.VMEM((rows, depth), bf16)],
        after=after,
        flops=2 * rows * width * depth,
    )


def d_normed_body(d_ref, w_ref, inverse_ref, t0, t1, t2, t3, t4, gain_ref, *out_refs):
    for start in range(0, w_ref.shape[0], STEP):
        span = slice(start, start + STEP)
        full = lax.dot_general(
            d_ref[...], w_ref[span, :], (((1,), (1,)), ((), ())), preferred_element_type=f32
        )
        split_rows(full, out_refs, span)
        at = 0
        total = jnp.zeros((1, STEP), f32)
        for ref in (t0, t1, t2, t3, t4):
            rows = slice(at, at + ref.shape[0])
            at += ref.shape[0]
            term = full[rows] * (ref[:, span].astype(f32) * inverse_ref[rows])
            total += jnp.sum(term, axis=0, keepdims=True)
        gain_ref[:, span] = total


def d_normed_parts(d_qkv, w_qkv, tokens, inverse, after):
    rows, depth = d_qkv.shape
    width = w_qkv.shape[0]
    out = call(
        d_normed_body,
        [((1, width), f32)] + [((n, width), bf16) for n in PIECES],
        local=[d_qkv, w_qkv, inverse, *tokens],
        after=after,
        mib=32,
        flops=2 * rows * width * depth,
    )
    return out[0], out[1:]


def columns_of(ref, block):
    return ref[:, pl.ds(pl.multiple_of(block * 256, 256), 256)]


def products(left_a, right_a, left_b, right_b, store):
    turned = (((0,), (0,)), ((), ()))
    for at in range(0, left_a.shape[1], STEP):
        span = slice(at, at + STEP)
        store(
            span,
            lax.dot_general(left_a[:, span], right_a, turned, preferred_element_type=f32),
            lax.dot_general(left_b[:, span], right_b, turned, preferred_element_type=f32),
        )


def rights(place_ref, by_x, away, refs):
    half = 1 - place_ref[0] if away else place_ref[0]
    if by_x:
        normed, d_qkv = refs
        return normed, columns_of(d_qkv, 3 * half), normed, columns_of(d_qkv, 3 * half + 1)
    normed, d_qkv, scaled, attended = refs
    return normed, columns_of(d_qkv, 3 * half + 2), scaled, columns_of(attended, half)


def away_body(by_x, place_ref, *refs):
    out_ref = refs[-1]

    def store(span, first, second):
        out_ref[span, :256] = first.astype(bf16)
        out_ref[span, 256:] = second.astype(bf16)

    products(*rights(place_ref, by_x, True, refs[:-1]), store)


def here_body(by_x, copies, place_ref, *refs):
    total = refs[-1]
    out_refs = refs[-8:-1]
    come_ref = refs[-9]

    def store(span, first, second):
        if span.start == 0:
            copies[0].wait()
        total[span, :256] = first + come_ref[span, :256].astype(f32)
        total[span, 256:] = second + come_ref[span, 256:].astype(f32)

    products(*rights(place_ref, by_x, False, refs[:-9]), store)
    chip_rows = total.shape[0] // 16

    def take(start, rows):
        span = pl.ds(pl.multiple_of(start, 8), rows)
        return total[span, :].astype(bf16)

    for j in (2, 1, 3, 0):
        if by_x:
            start = (j ^ place_ref[1]) * (4 * chip_rows)
            if j == 0:
                out_refs[0][...] = take(start, 4 * chip_rows)
            else:
                out_refs[2 * j - 1][...] = take(start, 2 * chip_rows)
                out_refs[2 * j][...] = take(start + 2 * chip_rows, 2 * chip_rows)
        else:
            for x in range(4):
                part = take((x * 4 + (j ^ place_ref[2])) * chip_rows, chip_rows)
                if j == 0:
                    out_refs[0][x] = part
                else:
                    out_refs[2 * j - 1 + x // 2][x % 2] = part


def column_products(place, by_x, operands, come=None, after=()):
    depth, width = operands[0].shape
    flops = 2 * width * depth * 512
    if come is None:
        return call(
            functools.partial(away_body, by_x),
            [((width, 512), bf16)],
            [place],
            operands,
            after=after,
            flops=flops,
        )
    rows = width // 4
    shapes = [(rows, 512)] + [(rows // 2, 512)] * 6
    if not by_x:
        shapes = [(4, rows // 4, 512)] + [(2, rows // 4, 512)] * 6
    return call(
        functools.partial(here_body, by_x),
        [(shape, bf16) for shape in shapes],
        [place],
        operands,
        [come],
        [pltpu.VMEM((width, 512), f32)],
        after,
        flops=flops,
    )


def mid_body(along, copies, place_ref, own_ref, r1, r2, r3, r4, *rest):
    out_refs, total = rest[:7], rest[7]
    for copy in copies:
        copy.wait()
    half = r1.shape[0]
    for y in range(own_ref.shape[0]):
        one = r1[y] if y < half else r2[y - half]
        three = r3[y] if y < half else r4[y - half]
        total[y] = own_ref[y].astype(f32) + one.astype(f32) + three.astype(f32)
    split = out_refs[1].shape[0]
    for j in range(4):
        part = total[j ^ place_ref[along]].astype(bf16)
        if j == 0:
            out_refs[0][...] = part
        else:
            out_refs[2 * j - 1][...] = part[:split]
            out_refs[2 * j][...] = part[split:]


def regroup(along, place, own, ring):
    _, rows, columns = own.shape
    low = rows // 32 * 16
    counts = [rows] + [low, rows - low] * 3
    return call(
        functools.partial(mid_body, along),
        [((n, columns), bf16) for n in counts],
        [place],
        fetched=[own, *ring],
        scratch=[pltpu.VMEM(own.shape, f32)],
        mib=12,
    )


def last_body(copies, place_ref, *refs):
    here_ref, there_ref = refs[10:]
    rows = here_ref.shape[0]
    for copy in copies:
        copy.wait()
    for side in range(2):
        own, r1, r2, r3, r4 = refs[5 * side : 5 * side + 5]
        span = slice(512 * side, 512 * side + 512)
        one = jnp.concatenate([r1[...].astype(f32), r2[...].astype(f32)])
        three = jnp.concatenate([r3[...].astype(f32), r4[...].astype(f32)])
        total = own[...].astype(f32) + one + three
        first = place_ref[0] == 0
        here_ref[:, span] = jnp.where(first, total[:rows], total[rows:]).astype(bf16)
        there_ref[:, span] = jnp.where(first, total[rows:], total[:rows]).astype(bf16)


def last_sums(place, left, left_ring, right, right_ring):
    shape = ((left.shape[0] // 2, 1024), bf16)
    return call(
        last_body, [shape, shape], [place], fetched=[left, *left_ring, right, *right_ring], mib=12
    )


def join_body(place_ref, here_ref, there_ref, qkv_ref, out_ref):
    first = place_ref[0] == 0
    here, there = here_ref[...].astype(f32), there_ref[...].astype(f32)
    low = jnp.where(first, here, there)
    high = jnp.where(first, there, here)
    qkv_ref[:, :768] = low[:, :768].astype(bf16)
    qkv_ref[:, 768:] = high[:, :768].astype(bf16)
    out_ref[:256] = low[:, 768:].T.astype(bf16)
    out_ref[256:] = high[:, 768:].T.astype(bf16)


def join(place, here, there):
    rows = here.shape[0]
    return call(
        join_body, [((rows, 1536), bf16), ((512, rows), bf16)], [place], [here, there], mib=12
    )


def swap_vision(x, flip):
    return lax.ppermute(x, "vision", [(i, i ^ flip) for i in range(4)])


def swap_dp(x, flip):
    return lax.ppermute(x, "dp", [(i, i ^ flip) for i in range(32)])


def gather_ring(x, swap):
    half = x.shape[0] // 2
    one = swap(x, 1)
    three = swap(x, 3)
    two_low = swap(one[:half], 3)
    two_high = swap(three[half:], 1)
    return [x, one, two_low, two_high, three]


def add_body(a_ref, b_ref, c_ref, d_ref, first_ref, second_ref):
    first_ref[...] = (a_ref[...].astype(f32) + b_ref[...].astype(f32)).astype(bf16)
    second_ref[...] = (c_ref[...].astype(f32) + d_ref[...].astype(f32)).astype(bf16)


def scatter_ring(parts, swap, after):
    own, one_low, one_high, two_low, two_high, three_low, three_high = parts
    low = swap(two_low, 1)
    high = swap(two_high, 3)
    from_one_low = swap(one_low, 1)
    from_three_high = swap(three_high, 3)
    three_low, one_high = call(
        add_body,
        [(three_low.shape, bf16), (one_high.shape, bf16)],
        local=[three_low, low, one_high, high],
        after=after,
        mib=12,
    )
    from_three_low = swap(three_low, 3)
    from_one_high = swap(one_high, 1)
    return own, (from_one_low, from_one_high, from_three_low, from_three_high)


def sum_everywhere(x):
    for flip in (1, 2, 6, 8, 24):
        x = x + swap_dp(x, flip)
    for flip in (1, 3):
        x = x + swap_vision(x, flip)
    return x


def swap_x(x, flip):
    return swap_dp(x, flip * 8)


def swap_y(x, flip):
    return swap_dp(x, flip * 2)


def pick(x, index, axis=0):
    return lax.dynamic_index_in_dim(x, index, axis, keepdims=False)


def tables(dest, replica_rank, vision_rank):
    everyone = dest.reshape(32, 64)
    me = replica_rank * 4 + vision_rank
    row = lax.dynamic_index_in_dim(everyone, replica_rank, 0, keepdims=False)
    owner_vision = row // 16 % 4
    owner_replica = row // 64
    j = jnp.arange(64, dtype=jnp.int32)
    source = j // 16
    same = (
        (owner_vision[:, None] == owner_vision[None])
        & (source[:, None] == source[None])
        & (j[None] < j[:, None])
    )
    rank = jnp.sum(same.astype(jnp.int32), axis=1)
    arrival = (owner_vision ^ vision_rank) * 16 + (source ^ owner_vision) * 4 + rank
    order = (source ^ vision_rank) * 16 + j % 16

    def table(at, values, count):
        hit = at[None] == jnp.arange(count, dtype=jnp.int32)[:, None]
        return jnp.sum(jnp.where(hit, values[None], 0), axis=1)

    arrival_of_row = table(order, arrival, 64)
    row_of_arrival = table(arrival, order, 16)
    replica_of_held = table(arrival, owner_replica, 16)
    held_of_replica = table(replica_of_held, jnp.arange(16, dtype=jnp.int32), 32)
    slot_of_replica = jnp.sum(jnp.where(everyone // 16 == me, everyone % 16, 0), axis=1)
    hit = everyone[None] == (me * 16 + jnp.arange(16, dtype=jnp.int32))[:, None, None]
    replica_of_slot = jnp.sum(
        jnp.where(hit, jnp.arange(32, dtype=jnp.int32)[None, :, None], 0), axis=(1, 2)
    )
    return (
        arrival_of_row,
        row_of_arrival,
        replica_of_held,
        held_of_replica,
        slot_of_replica,
        replica_of_slot,
    )


def body(tokens, gain, w_qkv, w_out, b_out, scale, dest, d_owned):
    vision_rank = lax.axis_index("vision")
    replica_rank = lax.axis_index("dp")
    rows_dev, width = tokens.shape
    blocks_dev = rows_dev // BLOCK
    chip_rows = width // 16
    x_rank, y_rank, core = replica_rank // 8, replica_rank // 2 % 4, replica_rank % 2
    chip = jnp.stack([core, x_rank, y_rank])

    def blocks(x):
        return x.reshape(-1, BLOCK, width)

    def row(x):
        return x.reshape(1, width)

    def to_dp(x):
        return lax.all_to_all(x, "dp", split_axis=0, concat_axis=0, tiled=True)

    (
        arrival_of_row,
        row_of_arrival,
        replica_of_held,
        held_of_replica,
        slot_of_replica,
        replica_of_slot,
    ) = tables(dest, replica_rank, vision_rank)
    place = (arrival_of_row[:, None] * BLOCK + jnp.arange(BLOCK, dtype=jnp.int32)[None]).reshape(-1, 1)

    parts = gather_ring(tokens, swap_vision)
    back = to_dp(gather_blocks(slot_of_replica, blocks(d_owned)))
    d_held = gather_blocks(replica_of_held, back).reshape(rows_dev, width)
    d_parts = gather_ring(d_held, swap_vision)

    own_norm = norm(parts[:1], row(gain))
    neighbour_norm = norm([parts[1], parts[4]], row(gain))
    normed, inverse, qkv, attended = forward(
        own_norm, neighbour_norm, parts[2:4], row(gain), place, w_qkv, [d_held]
    )
    head_parts = project(attended, w_out, [d_parts[1], d_parts[4]])
    token_rows = jnp.concatenate(parts)
    scaled, d_qkv = backward(d_parts, row(scale), w_out, qkv, place, [head_parts[0]])
    own, ring = scatter_ring(head_parts, swap_vision, [d_qkv])

    x_first = [normed, d_qkv]
    y_first = [normed, d_qkv, scaled, attended]
    left_away = column_products(chip, True, x_first, after=[])
    right_away = column_products(chip, False, y_first, after=[left_away])
    left_come = swap_dp(left_away, 1)
    right_come = swap_dp(right_away, 1)
    local_gain, pieces = d_normed_parts(d_qkv, w_qkv, parts, inverse, [right_away])
    left = column_products(chip, True, x_first, left_come, [local_gain])
    right = column_products(chip, False, y_first, right_come, [left[0]])
    sends, scale_and_bias = make_output(
        row_of_arrival, held_of_replica, blocks(token_rows), blocks(d_held), blocks(own),
        [blocks(r) for r in ring], row(b_out), row(scale), [right[0]],
    )
    left, left_ring = scatter_ring(left, swap_x, [])
    right, right_ring = scatter_ring(right, swap_y, [])
    arrived = to_dp(sends)
    own, ring = scatter_ring(pieces, swap_vision, [])

    by_y = lambda x: x.reshape(-1, chip_rows, 512)
    left = regroup(2, chip, by_y(left), [by_y(r) for r in left_ring])
    right = regroup(1, chip, right, right_ring)
    here, there = last_sums(chip, *scatter_ring(left, swap_y, []), *scatter_ring(right, swap_x, []))
    d_wqkv, d_wout = join(chip, here, swap_dp(there, 1))

    sums = sum_everywhere(jnp.concatenate([local_gain, scale_and_bias]))
    y_owned = gather_blocks(replica_of_slot, arrived).reshape(rows_dev, width)
    d_own = [d_parts[0][:32], d_parts[1][32:64], d_parts[3][:32], d_parts[4][96:]]
    own_rows = arrival_of_row[:blocks_dev]
    own_rows = own_rows // 16 * 4 + own_rows % 4
    d_tokens = make_d_tokens(
        own_rows, blocks(tokens), blocks(jnp.concatenate(d_own)), blocks(own),
        [blocks(r) for r in ring], row(gain),
    ).reshape(rows_dev, width)
    return y_owned, d_tokens, d_wqkv, d_wout, sums[0], sums[1], sums[2]


def solution(mesh):
    placed = (
        P(("dp", "vision"), None),
        P(),
        P(None, "vision"),
        P("vision", None),
        P(),
        P(),
        P(),
        P(("dp", "vision"), None),
    )
    return jax.shard_map(
        body,
        mesh=mesh,
        in_specs=placed,
        out_specs=(
            P(("dp", "vision"), None),
            P(("dp", "vision"), None),
            P("dp", "vision"),
            P("vision", "dp"),
            P(),
            P(),
            P(),
        ),
        check_vma=False,
    )
```

```python
import functools

import jax
import jax.numpy as jnp
from jax import lax
from jax.experimental import pallas as pl
from jax.experimental.pallas import tpu as pltpu
from jax.sharding import PartitionSpec as P

HEAD_DIM = 128
TILE = 256
BLOCK = 8
EPSILON = 1e-06
bf16 = jnp.bfloat16
f32 = jnp.float32


BIG = 58
INDEX = pl.BlockSpec(memory_space=pltpu.SMEM)
LOCAL = pl.BlockSpec(memory_space=pltpu.VMEM)
PLACED = pl.BlockSpec(memory_space=pl.ANY)


def call(kernel, outs, index=(), local=(), fetched=(), scratch=(), after=(), placed=(), mib=16):
    fetched = [f if isinstance(f, tuple) else (f, 0, 1) for f in fetched]
    first, second, third, fourth = len(index), len(local), len(fetched), len(placed)

    def body(*refs):
        at = first + second
        left = list(refs[at : at + fourth])
        at += fourth
        sources = refs[at : at + third]
        at += third + len(after)
        results = refs[at : at + len(outs)]
        at += len(outs)
        buffers = refs[at : at + third]
        at += third
        copies = []
        if third:
            sems = refs[at]
            at += 1
            n = 0
            for source, buffer, (_, axis, count) in zip(sources, buffers, fetched):
                copies.append([])
                step = source.shape[axis] // count
                for part in range(count):
                    span = (slice(None),) * axis + (pl.ds(part * step, step),)
                    copy = pltpu.make_async_copy(source.at[span], buffer.at[span], sems.at[n])
                    copy.start()
                    copies[-1].append(copy)
                    n += 1
        given = list(refs[: first + second]) + left + list(buffers)
        if third:
            kernel(copies, *given, *results, *refs[at:])
        else:
            kernel(*given, *results, *refs[at:])

    scratch_shapes = [pltpu.VMEM(x.shape, x.dtype) for x, _, _ in fetched]
    if third:
        scratch_shapes.append(pltpu.SemaphoreType.DMA((sum(n for _, _, n in fetched),)))
    result = pl.pallas_call(
        body,
        out_shape=tuple(jax.ShapeDtypeStruct(*o) for o in outs),
        in_specs=[INDEX] * first + [LOCAL] * second + [PLACED] * (fourth + third + len(after)),
        out_specs=tuple([LOCAL] * len(outs)),
        scratch_shapes=scratch_shapes + list(scratch),
        compiler_params=pltpu.CompilerParams(vmem_limit_bytes=mib * 2**20),
    )(*index, *local, *placed, *[x for x, _, _ in fetched], *after)
    return result if len(outs) > 1 else result[0]


def wait(copies):
    for copy in copies:
        copy.wait()


def gather_body(index_ref, source_ref, *out_refs):
    at = 0
    for out_ref in out_refs:
        for i in range(out_ref.shape[0]):
            out_ref[i] = source_ref[index_ref[at]]
            at += 1


def gather_blocks(index, source, parts=1, after=(), mib=16):
    shape = (index.shape[0] // parts,) + source.shape[1:]
    return call(
        gather_body, [(shape, source.dtype)] * parts, [index], [source], after=after, mib=mib
    )


def output_body(
    row_ref, send_ref, bias_ref, scale_ref, held_ref, own_ref, come_ref, t0, t1, t2, t3,
    out_ref, sums_ref, token_ref, made, by_scale, by_bias, sems,
):
    quarter = t0.shape[0]
    more = [
        pltpu.make_async_copy(t, token_ref.at[pl.ds(k * quarter, quarter)], sems.at[k])
        for k, t in enumerate((t0, t1, t2, t3))
    ]
    for copy in more:
        copy.start()
    scale = scale_ref[...]
    bias = bias_ref[...]
    wait(more)
    for i in range(held_ref.shape[0]):
        projected = own_ref[i].astype(f32) + come_ref[i].astype(f32) + bias
        tokens = token_ref[row_ref[i]].astype(f32)
        made[i] = (tokens + scale * projected).astype(bf16)
        d_output = held_ref[i].astype(f32)
        if i == 0:
            by_scale[...] = d_output * projected
            by_bias[...] = d_output * scale
        else:
            by_scale[...] += d_output * projected
            by_bias[...] += d_output * scale
    sums_ref[0:1] = jnp.sum(by_scale[...], axis=0, keepdims=True)
    sums_ref[1:2] = jnp.sum(by_bias[...], axis=0, keepdims=True)
    for i in range(out_ref.shape[0]):
        out_ref[i] = made[send_ref[i]]


def make_output(rows, sends, tokens, held, own, come, bias, scale, after):
    count, _, width = held.shape
    return call(
        output_body,
        [((sends.shape[0], BLOCK, width), bf16), ((2, width), f32)],
        [rows, sends],
        [bias, scale, held, own, come],
        scratch=[
            pltpu.VMEM((4 * count, BLOCK, width), bf16),
            pltpu.VMEM((count, BLOCK, width), bf16),
            pltpu.VMEM((BLOCK, width), f32),
            pltpu.VMEM((BLOCK, width), f32),
            pltpu.SemaphoreType.DMA((4,)),
        ],
        after=after,
        placed=tokens,
        mib=20,
    )


def d_tokens_body(
    row_ref, place_ref, gain_ref, token_ref, own_ref, come_ref, d0, d1, d2, d3,
    out_ref, held, sems,
):
    gain = gain_ref[...]
    quarter = held.shape[0] // 4
    mine = pl.ds(place_ref[3] * quarter, quarter)
    more = [
        pltpu.make_async_copy(d.at[mine], held.at[pl.ds(k * quarter, quarter)], sems.at[k])
        for k, d in enumerate((d0, d1, d2, d3))
    ]
    for copy in more:
        copy.start()
    wait(more)
    for i in range(token_ref.shape[0]):
        tokens = token_ref[i].astype(f32)
        inverse = lax.rsqrt(jnp.mean(tokens * tokens, axis=-1, keepdims=True) + EPSILON)
        scaled = (own_ref[i].astype(f32) + come_ref[i].astype(f32)) * gain
        inner = jnp.mean(scaled * tokens, axis=-1, keepdims=True)
        d_output = held[row_ref[i]].astype(f32)
        out_ref[i] = (
            d_output + inverse * scaled - tokens * (inverse * inverse * inverse * inner)
        ).astype(bf16)


def make_d_tokens(rows, chip, tokens, d_parts, own, come, gain, after):
    return call(
        d_tokens_body,
        [(tokens.shape, bf16)],
        [rows, chip],
        [gain, tokens, own, come],
        scratch=[pltpu.VMEM(tokens.shape, bf16), pltpu.SemaphoreType.DMA((4,))],
        placed=d_parts,
        after=after,
        mib=12,
    )


def norm_rows(token_ref, gain, normed_ref, inverse_ref, start):
    rows = 32

    def some(k, _):
        tokens = token_ref[pl.ds(pl.multiple_of(k * rows, rows), rows), :].astype(f32)
        inverse = lax.rsqrt(jnp.mean(tokens * tokens, axis=-1, keepdims=True) + EPSILON)
        to = pl.ds(pl.multiple_of(start + k * rows, rows), rows)
        inverse_ref[to, :] = inverse
        normed_ref[to, :] = (tokens * inverse * gain).astype(bf16)
        return 0

    lax.fori_loop(0, token_ref.shape[0] // rows, some, 0)


def softmax_of(query, keys, factor):
    scores = (
        lax.dot_general(query, keys, (((1,), (1,)), ((), ())), preferred_element_type=f32) * factor
    )
    top = jnp.max(scores, axis=-1, keepdims=True)
    weights = jnp.exp(scores - top)
    return weights / jnp.sum(weights, axis=-1, keepdims=True)


def permutation(place_ref, rows):
    columns = lax.broadcasted_iota(jnp.int32, (rows, rows), 1)
    return (place_ref[...] == columns).astype(f32).astype(bf16)


def ring_place(place_ref, axis, k):
    return (place_ref[axis] + jnp.where(place_ref[0] == 0, 3 * k, k)) & 3


def forward_body(
    factor, copies, chip_ref, gain_ref, place_ref, t0, t1, t2, t3, w_ref,
    normed_ref, inverse_ref, qkv_ref, attended_ref, held,
):
    rows = normed_ref.shape[0]
    part = rows // 4

    gain = gain_ref[...]
    for k, tokens in enumerate((t0, t1, t2, t3)):
        start = pl.multiple_of(ring_place(chip_ref, 3, k) * part, part)
        norm_rows(tokens, gain, normed_ref, inverse_ref, start)
    for n in range(qkv_ref.shape[1] // 256):
        span = slice(n * 256, (n + 1) * 256)
        if n % 2 == 0:
            copies[0][n // 2].wait()
        qkv_ref[:, span] = jnp.dot(
            normed_ref[...], w_ref[:, span], preferred_element_type=f32
        ).astype(bf16)
    for h in range(qkv_ref.shape[1] // (3 * HEAD_DIM)):
        for t in range(rows // TILE):
            span = slice(t * TILE, (t + 1) * TILE)
            at = 3 * h * HEAD_DIM
            query = qkv_ref[span, at : at + HEAD_DIM]
            keys = qkv_ref[span, at + HEAD_DIM : at + 2 * HEAD_DIM]
            values = qkv_ref[span, at + 2 * HEAD_DIM : at + 3 * HEAD_DIM]
            probs = softmax_of(query, keys, factor).astype(bf16)
            held[span, h * HEAD_DIM : (h + 1) * HEAD_DIM] = jnp.dot(
                probs, values, preferred_element_type=f32
            ).astype(bf16)
    perm = permutation(place_ref, rows)
    attended_ref[...] = lax.dot_general(
        perm, held[...], (((0,), (0,)), ((), ())), preferred_element_type=f32
    ).astype(bf16)


def forward(chip, tokens, gain, place, w_qkv, after):
    width, columns = w_qkv.shape
    rows = place.shape[0]
    return call(
        functools.partial(forward_body, HEAD_DIM**-0.5),
        [
            ((rows, width), bf16),
            ((rows, 1), f32),
            ((rows, columns), bf16),
            ((rows, columns // 3), bf16),
        ],
        index=[chip],
        local=[gain, place, *tokens],
        fetched=[(w_qkv, 1, 3)],
        scratch=[pltpu.VMEM((rows, columns // 3), bf16)],
        after=after,
        mib=26,
    )


def split_rows(value, out_refs, span):
    rows = value.shape[0] // len(out_refs)
    for k, out_ref in enumerate(out_refs):
        out_ref[:, span] = value[k * rows : (k + 1) * rows].astype(out_ref.dtype)


STEP = 640


def head_body(copies, attended_ref, w_ref, *out_refs):
    for n, at in enumerate(range(0, w_ref.shape[1], STEP)):
        span = slice(at, at + STEP)
        copies[0][n].wait()
        full = jnp.dot(attended_ref[...], w_ref[:, span], preferred_element_type=f32)
        split_rows(full, out_refs, span)


def project(attended, w_out, after):
    rows, depth = attended.shape
    width = w_out.shape[1]
    return call(
        head_body,
        [((rows // 4, width), bf16)] * 4,
        local=[attended],
        fetched=[(w_out, 1, width // STEP)],
        after=after,
        mib=12,
    )


def back_body(
    factor, copies, scale_ref, qkv_ref, place_ref, d0, d1, d2, d3, w_ref, scaled_ref, out_ref, held
):
    rows = qkv_ref.shape[0]
    at = 0
    for ref in (d0, d1, d2, d3):
        scaled_ref[at : at + ref.shape[0]] = (ref[...].astype(f32) * scale_ref[...]).astype(bf16)
        at += ref.shape[0]
    wait(copies[0])
    total = lax.dot_general(
        scaled_ref[...], w_ref[...], (((1,), (1,)), ((), ())), preferred_element_type=f32
    ).astype(bf16)
    perm = permutation(place_ref, rows)
    held[...] = jnp.dot(perm, total, preferred_element_type=f32).astype(bf16)
    for h in range(qkv_ref.shape[1] // (3 * HEAD_DIM)):
        for t in range(rows // TILE):
            span = slice(t * TILE, (t + 1) * TILE)
            at = 3 * h * HEAD_DIM
            query = qkv_ref[span, at : at + HEAD_DIM]
            keys = qkv_ref[span, at + HEAD_DIM : at + 2 * HEAD_DIM]
            values = qkv_ref[span, at + 2 * HEAD_DIM : at + 3 * HEAD_DIM]
            d_att = held[span, h * HEAD_DIM : (h + 1) * HEAD_DIM]
            probs = softmax_of(query, keys, factor)
            d_probs = lax.dot_general(
                d_att, values, (((1,), (1,)), ((), ())), preferred_element_type=f32
            )
            d_values = lax.dot_general(
                probs.astype(bf16), d_att, (((0,), (0,)), ((), ())), preferred_element_type=f32
            )
            inner = jnp.sum(probs * d_probs, axis=-1, keepdims=True)
            d_scores = (probs * (d_probs - inner) * factor).astype(bf16)
            d_query = jnp.dot(d_scores, keys, preferred_element_type=f32)
            d_keys = lax.dot_general(
                d_scores, query, (((0,), (0,)), ((), ())), preferred_element_type=f32
            )
            out_ref[span, at : at + HEAD_DIM] = d_query.astype(bf16)
            out_ref[span, at + HEAD_DIM : at + 2 * HEAD_DIM] = d_keys.astype(bf16)
            out_ref[span, at + 2 * HEAD_DIM : at + 3 * HEAD_DIM] = d_values.astype(bf16)


def backward(parts, scale, w_out, qkv, place, after):
    depth, width = w_out.shape
    rows, columns = qkv.shape
    return call(
        functools.partial(back_body, HEAD_DIM**-0.5),
        [((rows, width), bf16), ((rows, columns), bf16)],
        local=[scale, qkv, place, *parts],
        fetched=[w_out],
        scratch=[pltpu.VMEM((rows, depth), bf16)],
        after=after,
        mib=20,
    )


def d_normed_body(
    copies, chip_ref, d_ref, inverse_ref, t0, t1, t2, t3, w_ref, gain_ref, *refs
):
    out_refs, turned = refs[:4], refs[4]
    rows = t0.shape[0]
    inverses = []
    for k in range(4):
        at = pl.ds(pl.multiple_of(ring_place(chip_ref, 3, k) * rows, rows), rows)
        turned[k * rows : (k + 1) * rows] = d_ref[at, :]
        inverses.append(inverse_ref[at, :])
    for n, start in enumerate(range(0, w_ref.shape[0], STEP)):
        span = slice(start, start + STEP)
        copies[4][n].wait()
        full = lax.dot_general(
            turned[...], w_ref[span, :], (((1,), (1,)), ((), ())), preferred_element_type=f32
        )
        split_rows(full, out_refs, span)
        if n == 0:
            for each in copies[:4]:
                wait(each)
        total = jnp.zeros((1, STEP), f32)
        for k, ref in enumerate((t0, t1, t2, t3)):
            term = full[k * rows : (k + 1) * rows] * (ref[:, span].astype(f32) * inverses[k])
            total += jnp.sum(term, axis=0, keepdims=True)
        gain_ref[:, span] = total


def d_normed_parts(chip, d_qkv, w_qkv, tokens, inverse, after):
    rows, depth = d_qkv.shape
    width = w_qkv.shape[0]
    out = call(
        d_normed_body,
        [((1, width), f32)] + [((rows // 4, width), bf16)] * 4,
        [chip],
        [d_qkv, inverse],
        [*tokens, (w_qkv, 0, width // STEP)],
        [pltpu.VMEM(d_qkv.shape, bf16)],
        after,
        mib=26,
    )
    return out[0], out[1:]


def columns_of(ref, block):
    return ref[:, pl.ds(pl.multiple_of(block * 256, 256), 256)]


def products(left_a, right_a, left_b, right_b, store):
    turned = (((0,), (0,)), ((), ()))
    for at in range(0, left_a.shape[1], STEP):
        span = slice(at, at + STEP)
        store(
            span,
            lax.dot_general(left_a[:, span], right_a, turned, preferred_element_type=f32),
            lax.dot_general(left_b[:, span], right_b, turned, preferred_element_type=f32),
        )


def rights(place_ref, by_x, away, refs):
    half = 1 - place_ref[0] if away else place_ref[0]
    if by_x:
        normed, d_qkv = refs
        return normed, columns_of(d_qkv, 3 * half), normed, columns_of(d_qkv, 3 * half + 1)
    normed, d_qkv, scaled, attended = refs
    return normed, columns_of(d_qkv, 3 * half + 2), scaled, columns_of(attended, half)


def away_body(by_x, place_ref, *refs):
    out_ref = refs[-1]

    def store(span, first, second):
        out_ref[span, :256] = first.astype(bf16)
        out_ref[span, 256:] = second.astype(bf16)

    products(*rights(place_ref, by_x, True, refs[:-1]), store)


def here_body(by_x, copies, place_ref, *refs):
    out_refs, total = refs[-5:-1], refs[-1]
    come_ref = refs[-6]

    def store(span, first, second):
        if span.start == 0:
            wait(copies[0])
        total[span, :256] = first + come_ref[span, :256].astype(f32)
        total[span, 256:] = second + come_ref[span, 256:].astype(f32)

    products(*rights(place_ref, by_x, False, refs[:-6]), store)
    chip_rows = total.shape[0] // 16
    for k in (1, 2, 3, 0):
        for i in range(4):
            ring = ring_place(place_ref, 1 if by_x else 2, k)
            at = (4 * ring + i if by_x else 4 * i + ring) * chip_rows
            out_refs[k][i] = total[pl.ds(pl.multiple_of(at, 8), chip_rows), :].astype(bf16)


def column_products(place, by_x, operands, come=None, after=()):
    depth, width = operands[0].shape
    if come is None:
        return call(
            functools.partial(away_body, by_x),
            [((width, 512), bf16)],
            [place],
            operands,
            after=after,
            mib=16,
        )
    return call(
        functools.partial(here_body, by_x),
        [((4, width // 16, 512), bf16)] * 4,
        [place],
        operands,
        [come],
        [pltpu.VMEM((width, 512), f32)],
        after,
        mib=26,
    )


def mid_body(along, place_ref, own_ref, come_ref, *refs):
    out_refs, total = refs[:4], refs[4]
    for i in range(own_ref.shape[0]):
        total[i] = own_ref[i].astype(f32) + come_ref[i].astype(f32)
    for k in range(4):
        out_refs[k][...] = total[ring_place(place_ref, along, k)].astype(bf16)


def regroup(along, place, own, come, after):
    return call(
        functools.partial(mid_body, along),
        [(own.shape[1:], bf16)] * 4,
        [place],
        [own, come],
        scratch=[pltpu.VMEM(own.shape, f32)],
        after=after,
        mib=12,
    )


def last_body(place_ref, *refs):
    here_ref, there_ref = refs[8:]
    rows = here_ref.shape[0]
    for side in range(2):
        span = slice(512 * side, 512 * side + 512)
        total = sum(ref[...].astype(f32) for ref in refs[4 * side : 4 * side + 4])
        first = place_ref[0] == 0
        here_ref[:, span] = jnp.where(first, total[:rows], total[rows:]).astype(bf16)
        there_ref[:, span] = jnp.where(first, total[rows:], total[:rows]).astype(bf16)


def last_sums(place, left, right, after):
    shape = ((left[0].shape[0] // 2, 1024), bf16)
    return call(last_body, [shape, shape], [place], [*left, *right], after=after, mib=12)


def join_body(place_ref, here_ref, there_ref, qkv_ref, out_ref):
    first = place_ref[0] == 0
    here, there = here_ref[...].astype(f32), there_ref[...].astype(f32)
    low = jnp.where(first, here, there)
    high = jnp.where(first, there, here)
    qkv_ref[:, :768] = low[:, :768].astype(bf16)
    qkv_ref[:, 768:] = high[:, :768].astype(bf16)
    out_ref[:256] = low[:, 768:].T.astype(bf16)
    out_ref[256:] = high[:, 768:].T.astype(bf16)


def join(place, here, there, after):
    rows = here.shape[0]
    return call(
        join_body, [((rows, 1536), bf16), ((512, rows), bf16)], [place], [here, there], after=after, mib=12
    )


def swap_vision(x, flip):
    return lax.ppermute(x, "vision", [(i, i ^ flip) for i in range(4)])


def swap_dp(x, flip):
    return lax.ppermute(x, "dp", [(i, i ^ flip) for i in range(32)])


def pass_on(x, ring, steps=1):
    pairs = []
    for i in range(128):
        at = {"x": i // 32, "y": i // 8 % 4, "core": i // 4 % 2, "vision": i % 4}
        at[ring] = (at[ring] + (steps if at["core"] == 0 else -steps)) % 4
        pairs.append((i, at["x"] * 32 + at["y"] * 8 + at["core"] * 4 + at["vision"]))
    return lax.ppermute(x, ("dp", "vision"), pairs)


def add_body(a_ref, b_ref, out_ref):
    out_ref[...] = (a_ref[...].astype(f32) + b_ref[...].astype(f32)).astype(out_ref.dtype)


def add(a, b, after, mib=8):
    return call(add_body, [(a.shape, a.dtype)], local=[a, b], after=after, mib=mib)


def hold_body(x_ref, out_ref):
    out_ref[...] = x_ref[...]


def hold(x, after):
    return call(hold_body, [(x.shape, x.dtype)], local=[x], after=after, mib=8)


def scatter_direct(parts, ring):
    return [parts[0]] + [pass_on(parts[k], ring, 4 - k) for k in (1, 2, 3)]


def tables(dest, replica_rank, vision_rank):
    everyone = dest.reshape(32, 64)
    me = replica_rank * 4 + vision_rank
    row = lax.dynamic_index_in_dim(everyone, replica_rank, 0, keepdims=False)
    owner_vision = row // 16 % 4
    owner_replica = row // 64
    j = jnp.arange(64, dtype=jnp.int32)
    source = j // 16
    same = (
        (owner_vision[:, None] == owner_vision[None])
        & (source[:, None] == source[None])
        & (j[None] < j[:, None])
    )
    rank = jnp.sum(same.astype(jnp.int32), axis=1)
    way = jnp.where(replica_rank % 2 == 0, 3, 1)

    def steps(vision):
        return (way * (vision - vision_rank + 4)) % 4

    arrival = steps(owner_vision) * 16 + source * 4 + rank

    def table(at, values, count):
        hit = at[None] == jnp.arange(count, dtype=jnp.int32)[:, None]
        return jnp.sum(jnp.where(hit, values[None], 0), axis=1)

    row_of_held = table(arrival, steps(source) * 16 + j % 16, 16)
    replica_of_held = table(arrival, owner_replica, 16)
    held_of_replica = table(replica_of_held, jnp.arange(16, dtype=jnp.int32), 32)
    slot_of_replica = jnp.sum(jnp.where(everyone // 16 == me, everyone % 16, 0), axis=1)
    hit = everyone[None] == (me * 16 + jnp.arange(16, dtype=jnp.int32))[:, None, None]
    replica_of_slot = jnp.sum(
        jnp.where(hit, jnp.arange(32, dtype=jnp.int32)[None, :, None], 0), axis=(1, 2)
    )
    own = lax.dynamic_slice_in_dim(arrival, vision_rank * 16, 16)
    return (
        arrival,
        row_of_held,
        replica_of_held,
        held_of_replica,
        slot_of_replica,
        replica_of_slot,
        own // 16 * 4 + own % 4,
    )


def body(tokens, gain, w_qkv, w_out, b_out, scale, dest, d_owned):
    vision_rank = lax.axis_index("vision")
    replica_rank = lax.axis_index("dp")
    rows_dev, width = tokens.shape
    x_rank, y_rank, core = replica_rank // 8, replica_rank // 2 % 4, replica_rank % 2
    chip = jnp.stack([core, x_rank, y_rank, vision_rank])

    def blocks(x):
        return x.reshape(-1, BLOCK, width)

    def row(x):
        return x.reshape(1, width)

    def to_dp(x):
        return lax.all_to_all(x, "dp", split_axis=0, concat_axis=0, tiled=True)

    (
        arrival,
        row_of_held,
        replica_of_held,
        held_of_replica,
        slot_of_replica,
        replica_of_slot,
        own_rows,
    ) = tables(dest, replica_rank, vision_rank)
    place = (arrival[:, None] * BLOCK + jnp.arange(BLOCK, dtype=jnp.int32)[None]).reshape(-1, 1)

    send_back = gather_blocks(slot_of_replica, blocks(d_owned))
    back = to_dp(send_back)
    parts = [tokens, pass_on(tokens, "vision")]
    parts.append(pass_on(parts[1], "vision"))
    second = hold(parts[2], [send_back])
    parts.append(pass_on(second, "vision"))
    d_held = gather_blocks(replica_of_held, back, after=[second])
    d_parts = [d_held.reshape(rows_dev, width)]
    d_parts.append(pass_on(d_parts[0], "vision"))

    normed, inverse, qkv, attended = forward(chip, parts, row(gain), place, w_qkv, [d_held])
    d_parts.append(pass_on(hold(d_parts[1], [attended]), "vision"))
    head = project(attended, w_out, [d_parts[1]])
    d_parts.append(pass_on(hold(d_parts[2], [head[0]]), "vision"))
    first = hold(head[1], [d_parts[3]])
    head_come = pass_on(first, "vision")
    scaled, d_qkv = backward(d_parts, row(scale), w_out, qkv, place, [first])
    x_first = [normed, d_qkv]
    y_first = [normed, d_qkv, scaled, attended]
    left_away = column_products(chip, True, x_first)
    left_come = swap_dp(left_away, 1)
    total = add(head[2], head_come, [left_away], 8)
    head_come = pass_on(total, "vision")
    right_away = column_products(chip, False, y_first, after=[total])
    right_come = swap_dp(right_away, 1)
    left = column_products(chip, True, x_first, left_come, [right_away])
    left_now = pass_on(left[1], "x")
    right = column_products(chip, False, y_first, right_come, [left[0]])
    right_now = pass_on(right[1], "y")
    total = add(head[3], head_come, [right[0]], 8)
    head_come = pass_on(total, "vision")
    local_gain, pieces = d_normed_parts(chip, d_qkv, w_qkv, parts, inverse, [total])
    normed_now = pass_on(pieces[1], "vision")
    total = add(left[2], left_now, [pieces[0]])
    left_now = pass_on(total, "x")
    total = add(right[2], right_now, [total])
    right_now = pass_on(total, "y")
    sends, scale_and_bias = make_output(
        row_of_held, held_of_replica, [blocks(p) for p in parts], d_held, blocks(head[0]),
        blocks(head_come), row(b_out), row(scale), [total],
    )
    arrived = to_dp(sends)
    sums = jnp.concatenate([local_gain, scale_and_bias])
    sums_come = swap_dp(sums, 1)
    total = add(pieces[2], normed_now, [sends])
    normed_now = pass_on(total, "vision")
    sums = add(sums, sums_come, [total])
    sums_come = swap_vision(sums, 1)
    total = add(left[3], left_now, [sums])
    left_now = pass_on(total, "x")
    total = add(right[3], right_now, [total])
    right_now = pass_on(total, "y")
    sums = add(sums, sums_come, [total])
    sums_come = swap_vision(sums, 3)
    total = add(pieces[3], normed_now, [sums])
    normed_now = pass_on(total, "vision")
    left = regroup(2, chip, left[0], left_now, [total])
    left = scatter_direct(left, "y")
    sums = add(sums, sums_come, [left[0]])
    sums_come = swap_dp(sums, 8)
    right = regroup(1, chip, right[0], right_now, [sums])
    right = scatter_direct(right, "x")
    sums = add(sums, sums_come, [right[0]])
    sums_come = swap_dp(sums, 24)
    d_tokens = make_d_tokens(
        own_rows, chip, blocks(tokens), [blocks(d) for d in d_parts], blocks(pieces[0]),
        blocks(normed_now), row(gain), [sums],
    ).reshape(rows_dev, width)
    sums = add(sums, sums_come, [d_tokens])
    sums_come = swap_dp(sums, 2)
    here, there = last_sums(chip, left, right, [sums])
    there = swap_dp(there, 1)
    sums = add(sums, sums_come, [here])
    sums_come = swap_dp(sums, 6)
    y_owned = gather_blocks(replica_of_slot, arrived, after=[sums], mib=12)
    y_owned = y_owned.reshape(rows_dev, width)
    d_wqkv, d_wout = join(chip, here, there, [y_owned])
    sums = add(sums, sums_come, [d_wqkv])
    return y_owned, d_tokens, d_wqkv, d_wout, sums[0], sums[1], sums[2]


def solution(mesh):
    placed = (
        P(("dp", "vision"), None),
        P(),
        P(None, "vision"),
        P("vision", None),
        P(),
        P(),
        P(),
        P(("dp", "vision"), None),
    )
    return jax.shard_map(
        body,
        mesh=mesh,
        in_specs=placed,
        out_specs=(
            P(("dp", "vision"), None),
            P(("dp", "vision"), None),
            P("dp", "vision"),
            P("vision", "dp"),
            P(),
            P(),
            P(),
        ),
        check_vma=False,
    )
```

```python
import functools

import jax
import jax.numpy as jnp
from jax import lax
from jax.experimental import pallas as pl
from jax.experimental.pallas import tpu as pltpu
from jax.sharding import PartitionSpec as P

HEAD_DIM = 128
TILE = 256
BLOCK = 8
EPSILON = 1e-06
bf16 = jnp.bfloat16
f32 = jnp.float32


FORWARD = 50
INDEX = pl.BlockSpec(memory_space=pltpu.SMEM)
LOCAL = pl.BlockSpec(memory_space=pltpu.VMEM)
PLACED = pl.BlockSpec(memory_space=pl.ANY)


def call(kernel, outs, index=(), local=(), fetched=(), scratch=(), after=(), placed=(), mib=16):
    fetched = [f if isinstance(f, tuple) else (f, 0, 1) for f in fetched]
    first, second, third, fourth = len(index), len(local), len(fetched), len(placed)

    def body(*refs):
        at = first + second
        left = list(refs[at : at + fourth])
        at += fourth
        sources = refs[at : at + third]
        at += third + len(after)
        results = refs[at : at + len(outs)]
        at += len(outs)
        buffers = refs[at : at + third]
        at += third
        copies = []
        if third:
            sems = refs[at]
            at += 1
            n = 0
            for source, buffer, (_, axis, count) in zip(sources, buffers, fetched):
                copies.append([])
                step = source.shape[axis] // count
                for part in range(count):
                    span = (slice(None),) * axis + (pl.ds(part * step, step),)
                    copy = pltpu.make_async_copy(source.at[span], buffer.at[span], sems.at[n])
                    copy.start()
                    copies[-1].append(copy)
                    n += 1
        given = list(refs[: first + second]) + left + list(buffers)
        if third:
            kernel(copies, *given, *results, *refs[at:])
        else:
            kernel(*given, *results, *refs[at:])

    scratch_shapes = [pltpu.VMEM(x.shape, x.dtype) for x, _, _ in fetched]
    if third:
        scratch_shapes.append(pltpu.SemaphoreType.DMA((sum(n for _, _, n in fetched),)))
    result = pl.pallas_call(
        body,
        out_shape=tuple(jax.ShapeDtypeStruct(*o) for o in outs),
        in_specs=[INDEX] * first + [LOCAL] * second + [PLACED] * (fourth + third + len(after)),
        out_specs=tuple([LOCAL] * len(outs)),
        scratch_shapes=scratch_shapes + list(scratch),
        compiler_params=pltpu.CompilerParams(vmem_limit_bytes=mib * 2**20),
        cost_estimate=pl.CostEstimate(flops=1, bytes_accessed=1, transcendentals=0),
    )(*index, *local, *placed, *[x for x, _, _ in fetched], *after)
    return result if len(outs) > 1 else result[0]


def wait(copies):
    for copy in copies:
        copy.wait()


def gather_body(index_ref, source_ref, *out_refs):
    at = 0
    for out_ref in out_refs:
        for i in range(out_ref.shape[0]):
            out_ref[i] = source_ref[index_ref[at]]
            at += 1


def gather_blocks(index, source, parts=1, after=(), mib=16):
    shape = (index.shape[0] // parts,) + source.shape[1:]
    return call(
        gather_body, [(shape, source.dtype)] * parts, [index], [source], after=after, mib=mib
    )


def three(own_ref, near_ref, far_ref, i):
    return own_ref[i].astype(f32) + near_ref[i].astype(f32) + far_ref[i].astype(f32)


def output_body(
    row_ref, send_ref, bias_ref, scale_ref, held_ref, own_ref, near_ref, far_ref, t0, t1, t23,
    out_ref, sums_ref, token_ref, made, by_scale, by_bias, sems,
):
    quarter = t0.shape[0]
    more = [
        pltpu.make_async_copy(t, token_ref.at[pl.ds(k * quarter, quarter)], sems.at[k])
        for k, t in enumerate((t0, t1, t23.at[pl.ds(quarter, quarter)], t23.at[pl.ds(0, quarter)]))
    ]
    for copy in more:
        copy.start()
    scale = scale_ref[...]
    bias = bias_ref[...]
    wait(more)
    for i in range(held_ref.shape[0]):
        projected = three(own_ref, near_ref, far_ref, i) + bias
        tokens = token_ref[row_ref[i]].astype(f32)
        made[i] = (tokens + scale * projected).astype(bf16)
        d_output = held_ref[i].astype(f32)
        if i == 0:
            by_scale[...] = d_output * projected
            by_bias[...] = d_output * scale
        else:
            by_scale[...] += d_output * projected
            by_bias[...] += d_output * scale
    sums_ref[0:1] = jnp.sum(by_scale[...], axis=0, keepdims=True)
    sums_ref[1:2] = jnp.sum(by_bias[...], axis=0, keepdims=True)
    for i in range(out_ref.shape[0]):
        out_ref[i] = made[send_ref[i]]


def make_output(rows, sends, tokens, held, own, near, far, bias, scale, after):
    count, _, width = held.shape
    return call(
        output_body,
        [((sends.shape[0], BLOCK, width), bf16), ((2, width), f32)],
        [rows, sends],
        [bias, scale, held, own, near, far],
        scratch=[
            pltpu.VMEM((4 * count, BLOCK, width), bf16),
            pltpu.VMEM((count, BLOCK, width), bf16),
            pltpu.VMEM((BLOCK, width), f32),
            pltpu.VMEM((BLOCK, width), f32),
            pltpu.SemaphoreType.DMA((4,)),
        ],
        after=after,
        placed=tokens,
        mib=20,
    )


def d_tokens_body(
    row_ref, place_ref, gain_ref, token_ref, own_ref, near_ref, far_ref, d0, d1, d23,
    out_ref, held, sems,
):
    gain = gain_ref[...]
    quarter = held.shape[0] // 4
    mine = place_ref[3] * quarter
    more = [
        pltpu.make_async_copy(
            d.at[pl.ds(at + mine, quarter)], held.at[pl.ds(k * quarter, quarter)], sems.at[k]
        )
        for k, (d, at) in enumerate(((d0, 0), (d1, 0), (d23, 4 * quarter), (d23, 0)))
    ]
    for copy in more:
        copy.start()
    wait(more)
    for i in range(token_ref.shape[0]):
        tokens = token_ref[i].astype(f32)
        inverse = lax.rsqrt(jnp.mean(tokens * tokens, axis=-1, keepdims=True) + EPSILON)
        scaled = three(own_ref, near_ref, far_ref, i) * gain
        inner = jnp.mean(scaled * tokens, axis=-1, keepdims=True)
        d_output = held[row_ref[i]].astype(f32)
        out_ref[i] = (
            d_output + inverse * scaled - tokens * (inverse * inverse * inverse * inner)
        ).astype(bf16)


def make_d_tokens(rows, chip, tokens, d_parts, own, near, far, gain, after):
    return call(
        d_tokens_body,
        [(tokens.shape, bf16)],
        [rows, chip],
        [gain, tokens, own, near, far],
        scratch=[pltpu.VMEM(tokens.shape, bf16), pltpu.SemaphoreType.DMA((4,))],
        placed=d_parts,
        after=after,
        mib=12,
    )


def norm_rows(token_ref, first, count, gain, normed_ref, inverse_ref, start):
    rows = 32

    def some(k, _):
        at = pl.ds(pl.multiple_of(first + k * rows, rows), rows)
        tokens = token_ref[at, :].astype(f32)
        inverse = lax.rsqrt(jnp.mean(tokens * tokens, axis=-1, keepdims=True) + EPSILON)
        to = pl.ds(pl.multiple_of(start + k * rows, rows), rows)
        inverse_ref[to, :] = inverse
        normed_ref[to, :] = (tokens * inverse * gain).astype(bf16)
        return 0

    lax.fori_loop(0, count // rows, some, 0)


def softmax_of(query, keys, factor):
    scores = (
        lax.dot_general(query, keys, (((1,), (1,)), ((), ())), preferred_element_type=f32) * factor
    )
    top = jnp.max(scores, axis=-1, keepdims=True)
    weights = jnp.exp(scores - top)
    return weights / jnp.sum(weights, axis=-1, keepdims=True)


def permutation(place_ref, rows):
    columns = lax.broadcasted_iota(jnp.int32, (rows, rows), 1)
    return (place_ref[...] == columns).astype(f32).astype(bf16)


def ring_place(place_ref, axis, k):
    core = place_ref[0]
    return place_ref[axis] ^ (0, 1 + 2 * core, 2, 3 - 2 * core)[k]


def forward_body(
    copies, chip_ref, gain_ref, t0, t1, t23, w_ref, normed_ref, inverse_ref, qkv_ref
):
    rows = normed_ref.shape[0]
    part = rows // 4

    gain = gain_ref[...]
    for k, (tokens, at) in enumerate(((t0, 0), (t1, 0), (t23, part), (t23, 0))):
        start = pl.multiple_of(ring_place(chip_ref, 3, k) * part, part)
        norm_rows(tokens, at, part, gain, normed_ref, inverse_ref, start)
    for n in range(qkv_ref.shape[1] // 256):
        span = slice(n * 256, (n + 1) * 256)
        if n % 2 == 0:
            copies[0][n // 2].wait()
        qkv_ref[:, span] = jnp.dot(
            normed_ref[...], w_ref[:, span], preferred_element_type=f32
        ).astype(bf16)


def attend_body(factor, place_ref, qkv_ref, attended_ref, held):
    rows = qkv_ref.shape[0]
    for h in range(qkv_ref.shape[1] // (3 * HEAD_DIM)):
        for t in range(rows // TILE):
            span = slice(t * TILE, (t + 1) * TILE)
            at = 3 * h * HEAD_DIM
            query = qkv_ref[span, at : at + HEAD_DIM]
            keys = qkv_ref[span, at + HEAD_DIM : at + 2 * HEAD_DIM]
            values = qkv_ref[span, at + 2 * HEAD_DIM : at + 3 * HEAD_DIM]
            probs = softmax_of(query, keys, factor).astype(bf16)
            held[span, h * HEAD_DIM : (h + 1) * HEAD_DIM] = jnp.dot(
                probs, values, preferred_element_type=f32
            ).astype(bf16)
    perm = permutation(place_ref, rows)
    attended_ref[...] = lax.dot_general(
        perm, held[...], (((0,), (0,)), ((), ())), preferred_element_type=f32
    ).astype(bf16)


def forward(chip, tokens, gain, w_qkv, after):
    width, columns = w_qkv.shape
    rows = 4 * tokens[0].shape[0]
    return call(
        forward_body,
        [((rows, width), bf16), ((rows, 1), f32), ((rows, columns), bf16)],
        index=[chip],
        local=[gain, *tokens],
        fetched=[(w_qkv, 1, 3)],
        after=after,
        mib=FORWARD,
    )


def attend(qkv, place, after):
    rows, columns = qkv.shape
    return call(
        functools.partial(attend_body, HEAD_DIM**-0.5),
        [((rows, columns // 3), bf16)],
        local=[place, qkv],
        scratch=[pltpu.VMEM((rows, columns // 3), bf16)],
        after=after,
        mib=16,
    )


def split_rows(value, out_refs, span):
    at = 0
    for out_ref in out_refs:
        out_ref[:, span] = value[at : at + out_ref.shape[0]].astype(out_ref.dtype)
        at += out_ref.shape[0]


QUARTERS = (1, 2, 1)
STEP = 640


def head_body(copies, attended_ref, w_ref, *out_refs):
    for n, at in enumerate(range(0, w_ref.shape[1], STEP)):
        span = slice(at, at + STEP)
        copies[0][n].wait()
        full = jnp.dot(attended_ref[...], w_ref[:, span], preferred_element_type=f32)
        split_rows(full, out_refs, span)


def project(attended, w_out, after):
    rows, depth = attended.shape
    width = w_out.shape[1]
    return call(
        head_body,
        [((rows // 4 * n, width), bf16) for n in QUARTERS],
        local=[attended],
        fetched=[(w_out, 1, width // STEP)],
        after=after,
        mib=12,
    )


def back_body(
    factor, copies, scale_ref, qkv_ref, place_ref, d0, d1, d23, w_ref, scaled_ref, out_ref, held
):
    rows = qkv_ref.shape[0]
    part = rows // 4
    for k, (ref, at) in enumerate(((d0, 0), (d1, 0), (d23, part), (d23, 0))):
        term = ref[at : at + part].astype(f32) * scale_ref[...]
        scaled_ref[k * part : (k + 1) * part] = term.astype(bf16)
    wait(copies[0])
    total = lax.dot_general(
        scaled_ref[...], w_ref[...], (((1,), (1,)), ((), ())), preferred_element_type=f32
    ).astype(bf16)
    perm = permutation(place_ref, rows)
    held[...] = jnp.dot(perm, total, preferred_element_type=f32).astype(bf16)
    for h in range(qkv_ref.shape[1] // (3 * HEAD_DIM)):
        for t in range(rows // TILE):
            span = slice(t * TILE, (t + 1) * TILE)
            at = 3 * h * HEAD_DIM
            query = qkv_ref[span, at : at + HEAD_DIM]
            keys = qkv_ref[span, at + HEAD_DIM : at + 2 * HEAD_DIM]
            values = qkv_ref[span, at + 2 * HEAD_DIM : at + 3 * HEAD_DIM]
            d_att = held[span, h * HEAD_DIM : (h + 1) * HEAD_DIM]
            probs = softmax_of(query, keys, factor)
            d_probs = lax.dot_general(
                d_att, values, (((1,), (1,)), ((), ())), preferred_element_type=f32
            )
            d_values = lax.dot_general(
                probs.astype(bf16), d_att, (((0,), (0,)), ((), ())), preferred_element_type=f32
            )
            inner = jnp.sum(probs * d_probs, axis=-1, keepdims=True)
            d_scores = (probs * (d_probs - inner) * factor).astype(bf16)
            d_query = jnp.dot(d_scores, keys, preferred_element_type=f32)
            d_keys = lax.dot_general(
                d_scores, query, (((0,), (0,)), ((), ())), preferred_element_type=f32
            )
            out_ref[span, at : at + HEAD_DIM] = d_query.astype(bf16)
            out_ref[span, at + HEAD_DIM : at + 2 * HEAD_DIM] = d_keys.astype(bf16)
            out_ref[span, at + 2 * HEAD_DIM : at + 3 * HEAD_DIM] = d_values.astype(bf16)


def backward(parts, scale, w_out, qkv, place, after):
    depth, width = w_out.shape
    rows, columns = qkv.shape
    return call(
        functools.partial(back_body, HEAD_DIM**-0.5),
        [((rows, width), bf16), ((rows, columns), bf16)],
        local=[scale, qkv, place, *parts],
        fetched=[w_out],
        scratch=[pltpu.VMEM((rows, depth), bf16)],
        after=after,
        mib=20,
    )


def d_normed_body(
    copies, chip_ref, d_ref, inverse_ref, t0, t1, t23, w_ref, gain_ref, *refs
):
    out_refs, turned = refs[:3], refs[3]
    rows = t0.shape[0]
    inverses = []
    for k in range(4):
        at = pl.ds(pl.multiple_of(ring_place(chip_ref, 3, k) * rows, rows), rows)
        turned[k * rows : (k + 1) * rows] = d_ref[at, :]
        inverses.append(inverse_ref[at, :])
    for n, start in enumerate(range(0, w_ref.shape[0], STEP)):
        span = slice(start, start + STEP)
        copies[3][n].wait()
        full = lax.dot_general(
            turned[...], w_ref[span, :], (((1,), (1,)), ((), ())), preferred_element_type=f32
        )
        split_rows(full, out_refs, span)
        if n == 0:
            for each in copies[:3]:
                wait(each)
        total = jnp.zeros((1, STEP), f32)
        for k, (ref, at) in enumerate(((t0, 0), (t1, 0), (t23, rows), (t23, 0))):
            tokens = ref[at : at + rows, span].astype(f32)
            term = full[k * rows : (k + 1) * rows] * (tokens * inverses[k])
            total += jnp.sum(term, axis=0, keepdims=True)
        gain_ref[:, span] = total


def d_normed_parts(chip, d_qkv, w_qkv, tokens, inverse, after):
    rows, depth = d_qkv.shape
    width = w_qkv.shape[0]
    out = call(
        d_normed_body,
        [((1, width), f32)] + [((rows // 4 * n, width), bf16) for n in QUARTERS],
        [chip],
        [d_qkv, inverse],
        [*tokens, (w_qkv, 0, width // STEP)],
        [pltpu.VMEM(d_qkv.shape, bf16)],
        after,
        mib=26,
    )
    return out[0], out[1:]


def columns_of(ref, block):
    return ref[:, pl.ds(pl.multiple_of(block * 256, 256), 256)]


def products(left_a, right_a, left_b, right_b, store):
    turned = (((0,), (0,)), ((), ()))
    for at in range(0, left_a.shape[1], STEP):
        span = slice(at, at + STEP)
        store(
            span,
            lax.dot_general(left_a[:, span], right_a, turned, preferred_element_type=f32),
            lax.dot_general(left_b[:, span], right_b, turned, preferred_element_type=f32),
        )


def rights(place_ref, by_x, away, refs):
    half = 1 - place_ref[0] if away else place_ref[0]
    if by_x:
        normed, d_qkv = refs
        return normed, columns_of(d_qkv, 3 * half), normed, columns_of(d_qkv, 3 * half + 1)
    normed, d_qkv, scaled, attended = refs
    return normed, columns_of(d_qkv, 3 * half + 2), scaled, columns_of(attended, half)


def away_body(by_x, place_ref, *refs):
    out_ref = refs[-1]

    def store(span, first, second):
        out_ref[span, :256] = first.astype(bf16)
        out_ref[span, 256:] = second.astype(bf16)

    products(*rights(place_ref, by_x, True, refs[:-1]), store)


def here_body(by_x, place_ref, *refs):
    out_refs, total = refs[-4:-1], refs[-1]
    come_ref = refs[-5]

    def store(span, first, second):
        total[span, :256] = first + come_ref[span, :256].astype(f32)
        total[span, 256:] = second + come_ref[span, 256:].astype(f32)

    products(*rights(place_ref, by_x, False, refs[:-5]), store)
    chip_rows = total.shape[0] // 16
    for k in (1, 2, 3, 0):
        for i in range(4):
            ring = ring_place(place_ref, 1 if by_x else 2, k)
            at = (4 * ring + i if by_x else 4 * i + ring) * chip_rows
            part = total[pl.ds(pl.multiple_of(at, 8), chip_rows), :].astype(bf16)
            out_refs[(0, 1, 1, 2)[k]][4 * (k == 2) + i] = part


def column_products(place, by_x, operands, come=None, after=()):
    depth, width = operands[0].shape
    if come is None:
        return call(
            functools.partial(away_body, by_x),
            [((width, 512), bf16)],
            [place],
            operands,
            after=after,
            mib=16,
        )
    return call(
        functools.partial(here_body, by_x),
        [((4 * n, width // 16, 512), bf16) for n in QUARTERS],
        [place],
        [*operands, come],
        scratch=[pltpu.VMEM((width, 512), f32)],
        after=after,
        mib=26,
    )


def mid_body(along, place_ref, own_ref, near_ref, far_ref, *refs):
    out_refs, total = refs[:3], refs[3]
    for i in range(own_ref.shape[0]):
        total[i] = three(own_ref, near_ref, far_ref, i)
    for k in range(4):
        part = total[ring_place(place_ref, along, k)].astype(bf16)
        out_refs[(0, 1, 1, 2)[k]][1 if k == 2 else 0] = part


def regroup(along, place, own, near, far, after):
    return call(
        functools.partial(mid_body, along),
        [((n,) + own.shape[1:], bf16) for n in QUARTERS],
        [place],
        [own, near, far],
        scratch=[pltpu.VMEM(own.shape, f32)],
        after=after,
        mib=12,
    )


def last_body(place_ref, *refs):
    here_ref, there_ref = refs[6:]
    rows = here_ref.shape[0]
    for side in range(2):
        span = slice(512 * side, 512 * side + 512)
        total = three(*refs[3 * side : 3 * side + 3], 0)
        first = place_ref[0] == 0
        here_ref[:, span] = jnp.where(first, total[:rows], total[rows:]).astype(bf16)
        there_ref[:, span] = jnp.where(first, total[rows:], total[:rows]).astype(bf16)


def last_sums(place, left, right, after):
    shape = ((left[0].shape[1] // 2, 1024), bf16)
    return call(last_body, [shape, shape], [place], [*left, *right], after=after, mib=12)


def join_body(place_ref, here_ref, there_ref, qkv_ref, out_ref):
    first = place_ref[0] == 0
    here, there = here_ref[...].astype(f32), there_ref[...].astype(f32)
    low = jnp.where(first, here, there)
    high = jnp.where(first, there, here)
    qkv_ref[:, :768] = low[:, :768].astype(bf16)
    qkv_ref[:, 768:] = high[:, :768].astype(bf16)
    out_ref[:256] = low[:, 768:].T.astype(bf16)
    out_ref[256:] = high[:, 768:].T.astype(bf16)


def join(place, here, there, after):
    rows = here.shape[0]
    return call(
        join_body, [((rows, 1536), bf16), ((512, rows), bf16)], [place], [here, there], after=after, mib=12
    )


def swap_vision(x, flip):
    return lax.ppermute(x, "vision", [(i, i ^ flip) for i in range(4)])


def swap_dp(x, flip):
    return lax.ppermute(x, "dp", [(i, i ^ flip) for i in range(32)])


def pass_on(x, ring, second):
    pairs = []
    for i in range(128):
        at = {"x": i // 32, "y": i // 8 % 4, "core": i // 4 % 2, "vision": i % 4}
        at[ring] ^= 3 if (at["core"] == 0) == second else 1
        pairs.append((i, at["x"] * 32 + at["y"] * 8 + at["core"] * 4 + at["vision"]))
    return lax.ppermute(x, ("dp", "vision"), pairs)


def add_body(a_ref, b_ref, out_ref):
    out_ref[...] = (a_ref[...].astype(f32) + b_ref[...].astype(f32)).astype(out_ref.dtype)


def add(a, b, after, mib=8):
    return call(add_body, [(a.shape, a.dtype)], local=[a, b], after=after, mib=mib)


def hold_body(x_ref, out_ref):
    out_ref[...] = x_ref[...]


def hold(x, after):
    return call(hold_body, [(x.shape, x.dtype)], local=[x], after=after, mib=8)


def pair_body(a_ref, b_ref, out_ref):
    rows = a_ref.shape[0]
    out_ref[:rows] = a_ref[...]
    out_ref[rows:] = b_ref[...]


def pair(a, b, after):
    shape = (2 * a.shape[0],) + a.shape[1:]
    return call(pair_body, [(shape, a.dtype)], local=[a, b], after=after, mib=8)


def add_far_body(far_ref, near_ref, out_ref):
    rows = far_ref.shape[0]
    out_ref[...] = (far_ref[...].astype(f32) + near_ref[rows:].astype(f32)).astype(out_ref.dtype)


def add_far(far, near, after):
    return call(add_far_body, [(far.shape, far.dtype)], local=[far, near], after=after, mib=12)


def tables(dest, replica_rank, vision_rank):
    everyone = dest.reshape(32, 64)
    me = replica_rank * 4 + vision_rank
    row = lax.dynamic_index_in_dim(everyone, replica_rank, 0, keepdims=False)
    owner_vision = row // 16 % 4
    owner_replica = row // 64
    j = jnp.arange(64, dtype=jnp.int32)
    source = j // 16
    same = (
        (owner_vision[:, None] == owner_vision[None])
        & (source[:, None] == source[None])
        & (j[None] < j[:, None])
    )
    rank = jnp.sum(same.astype(jnp.int32), axis=1)
    way = jnp.where(replica_rank % 2 == 0, 1, 3)

    def steps(vision):
        return (way * (vision ^ vision_rank)) % 4

    arrival = steps(owner_vision) * 16 + source * 4 + rank

    def table(at, values, count):
        hit = at[None] == jnp.arange(count, dtype=jnp.int32)[:, None]
        return jnp.sum(jnp.where(hit, values[None], 0), axis=1)

    row_of_held = table(arrival, steps(source) * 16 + j % 16, 16)
    replica_of_held = table(arrival, owner_replica, 16)
    held_of_replica = table(replica_of_held, jnp.arange(16, dtype=jnp.int32), 32)
    slot_of_replica = jnp.sum(jnp.where(everyone // 16 == me, everyone % 16, 0), axis=1)
    hit = everyone[None] == (me * 16 + jnp.arange(16, dtype=jnp.int32))[:, None, None]
    replica_of_slot = jnp.sum(
        jnp.where(hit, jnp.arange(32, dtype=jnp.int32)[None, :, None], 0), axis=(1, 2)
    )
    own = lax.dynamic_slice_in_dim(arrival, vision_rank * 16, 16)
    return (
        arrival,
        row_of_held,
        replica_of_held,
        held_of_replica,
        slot_of_replica,
        replica_of_slot,
        own // 16 * 4 + own % 4,
    )


def body(tokens, gain, w_qkv, w_out, b_out, scale, dest, d_owned):
    vision_rank = lax.axis_index("vision")
    replica_rank = lax.axis_index("dp")
    rows_dev, width = tokens.shape
    x_rank, y_rank, core = replica_rank // 8, replica_rank // 2 % 4, replica_rank % 2
    chip = jnp.stack([core, x_rank, y_rank, vision_rank])

    def blocks(x):
        return x.reshape(-1, BLOCK, width)

    def row(x):
        return x.reshape(1, width)

    def to_dp(x):
        return lax.all_to_all(x, "dp", split_axis=0, concat_axis=0, tiled=True)

    (
        arrival,
        row_of_held,
        replica_of_held,
        held_of_replica,
        slot_of_replica,
        replica_of_slot,
        own_rows,
    ) = tables(dest, replica_rank, vision_rank)
    place = (arrival[:, None] * BLOCK + jnp.arange(BLOCK, dtype=jnp.int32)[None]).reshape(-1, 1)

    send_back = gather_blocks(slot_of_replica, blocks(d_owned))
    back = to_dp(send_back)
    near = pass_on(tokens, "vision", False)
    both = pair(tokens, near, [send_back])
    parts = [tokens, near, pass_on(both, "vision", True)]
    gain, scale, b_out = row(gain), row(scale), row(b_out)
    d_held = gather_blocks(replica_of_held, back, after=[both, place, gain])
    d_own = d_held.reshape(rows_dev, width)
    d_near = pass_on(d_own, "vision", False)

    normed, inverse, qkv = forward(chip, parts, gain, w_qkv, [d_held])
    both = pair(d_own, d_near, [qkv])
    attended = attend(qkv, place, [both])
    d_parts = [d_own, d_near, pass_on(both, "vision", True)]
    head = project(attended, w_out, [])
    first = hold(head[1], [d_parts[2]])
    head_near = pass_on(first, "vision", False)
    scaled, d_qkv = backward(d_parts, scale, w_out, qkv, place, [first])
    x_first = [normed, d_qkv]
    y_first = [normed, d_qkv, scaled, attended]
    left_away = column_products(chip, True, x_first)
    left_come = swap_dp(left_away, 1)
    right_away = column_products(chip, False, y_first, after=[left_away])
    right_come = swap_dp(right_away, 1)
    left = column_products(chip, True, x_first, left_come, [right_away])
    left_near = pass_on(left[1], "x", False)
    right = column_products(chip, False, y_first, right_come, [left[0]])
    right_near = pass_on(right[1], "y", False)
    total = add_far(head[2], head_near, [right[0]])
    head_far = pass_on(total, "vision", True)
    local_gain, pieces = d_normed_parts(chip, d_qkv, w_qkv, parts, inverse, [total])
    normed_near = pass_on(pieces[1], "vision", False)
    sends, scale_and_bias = make_output(
        row_of_held, held_of_replica, [blocks(p) for p in parts], d_held, blocks(head[0]),
        blocks(head_near), blocks(head_far), b_out, scale, [pieces[0]],
    )
    sums = jnp.concatenate([local_gain, scale_and_bias])
    sums_come = swap_dp(sums, 1)
    total = add_far(left[2], left_near, [sends])
    left_far = pass_on(total, "x", True)
    total = add_far(right[2], right_near, [total])
    right_far = pass_on(total, "y", True)
    sums = add(sums, sums_come, [total])
    sums_come = swap_vision(sums, 1)
    left = regroup(2, chip, left[0], left_near, left_far, [sums])
    left_near = pass_on(left[1], "y", False)
    sums = add(sums, sums_come, [left[0]])
    sums_come = swap_vision(sums, 3)
    right = regroup(1, chip, right[0], right_near, right_far, [sums])
    right_near = pass_on(right[1], "x", False)
    total = add_far(pieces[2], normed_near, [right[0]])
    normed_far = pass_on(total, "vision", True)
    sums = add(sums, sums_come, [total])
    sums_come = swap_dp(sums, 8)
    total = add_far(left[2], left_near, [sums])
    left_far = pass_on(total, "y", True)
    total = add_far(right[2], right_near, [total])
    right_far = pass_on(total, "x", True)
    sums = add(sums, sums_come, [total])
    sums_come = swap_dp(sums, 24)
    held = hold(sends, [sums])
    arrived = to_dp(held)
    d_tokens = make_d_tokens(
        own_rows, chip, blocks(tokens), [blocks(d) for d in d_parts], blocks(pieces[0]),
        blocks(normed_near), blocks(normed_far), gain, [held],
    ).reshape(rows_dev, width)
    sums = add(sums, sums_come, [d_tokens])
    sums_come = swap_dp(sums, 2)
    here, there = last_sums(
        chip, [left[0], left_near, left_far], [right[0], right_near, right_far], [sums]
    )
    there = swap_dp(there, 1)
    sums = add(sums, sums_come, [here])
    sums_come = swap_dp(sums, 6)
    d_wqkv, d_wout = join(chip, here, there, [sums])
    sums = add(sums, sums_come, [d_wqkv])
    y_owned = gather_blocks(replica_of_slot, arrived, after=[sums], mib=12)
    y_owned = y_owned.reshape(rows_dev, width)
    return y_owned, d_tokens, d_wqkv, d_wout, sums[0], sums[1], sums[2]


def solution(mesh):
    placed = (
        P(("dp", "vision"), None),
        P(),
        P(None, "vision"),
        P("vision", None),
        P(),
        P(),
        P(),
        P(("dp", "vision"), None),
    )
    return jax.shard_map(
        body,
        mesh=mesh,
        in_specs=placed,
        out_specs=(
            P(("dp", "vision"), None),
            P(("dp", "vision"), None),
            P("dp", "vision"),
            P("vision", "dp"),
            P(),
            P(),
            P(),
        ),
        check_vma=False,
    )
```

```python
import functools

import jax
import jax.numpy as jnp
from jax import lax
from jax.experimental import pallas as pl
from jax.experimental.pallas import tpu as pltpu
from jax.sharding import PartitionSpec as P

HEAD_DIM = 128
TILE = 256
BLOCK = 8
EPSILON = 1e-06
bf16 = jnp.bfloat16
f32 = jnp.float32


FORWARD = 50
INDEX = pl.BlockSpec(memory_space=pltpu.SMEM)
LOCAL = pl.BlockSpec(memory_space=pltpu.VMEM)
PLACED = pl.BlockSpec(memory_space=pl.ANY)


def call(kernel, outs, index=(), local=(), fetched=(), scratch=(), after=(), placed=(), mib=16):
    fetched = [f if isinstance(f, tuple) else (f, 0, 1) for f in fetched]
    first, second, third, fourth = len(index), len(local), len(fetched), len(placed)

    def body(*refs):
        at = first + second
        left = list(refs[at : at + fourth])
        at += fourth
        sources = refs[at : at + third]
        at += third + len(after)
        results = refs[at : at + len(outs)]
        at += len(outs)
        buffers = refs[at : at + third]
        at += third
        copies = []
        if third:
            sems = refs[at]
            at += 1
            n = 0
            for source, buffer, (_, axis, count) in zip(sources, buffers, fetched):
                copies.append([])
                step = source.shape[axis] // count
                for part in range(count):
                    span = (slice(None),) * axis + (pl.ds(part * step, step),)
                    copy = pltpu.make_async_copy(source.at[span], buffer.at[span], sems.at[n])
                    copy.start()
                    copies[-1].append(copy)
                    n += 1
        given = list(refs[: first + second]) + left + list(buffers)
        if third:
            kernel(copies, *given, *results, *refs[at:])
        else:
            kernel(*given, *results, *refs[at:])

    scratch_shapes = [pltpu.VMEM(x.shape, x.dtype) for x, _, _ in fetched]
    if third:
        scratch_shapes.append(pltpu.SemaphoreType.DMA((sum(n for _, _, n in fetched),)))
    result = pl.pallas_call(
        body,
        out_shape=tuple(jax.ShapeDtypeStruct(*o) for o in outs),
        in_specs=[INDEX] * first + [LOCAL] * second + [PLACED] * (fourth + third + len(after)),
        out_specs=tuple([LOCAL] * len(outs)),
        scratch_shapes=scratch_shapes + list(scratch),
        compiler_params=pltpu.CompilerParams(vmem_limit_bytes=mib * 2**20),
        cost_estimate=pl.CostEstimate(flops=1, bytes_accessed=1, transcendentals=0),
    )(*index, *local, *placed, *[x for x, _, _ in fetched], *after)
    return result if len(outs) > 1 else result[0]


def wait(copies):
    for copy in copies:
        copy.wait()


def gather_body(index_ref, source_ref, *out_refs):
    at = 0
    for out_ref in out_refs:
        for i in range(out_ref.shape[0]):
            out_ref[i] = source_ref[index_ref[at]]
            at += 1


def gather_blocks(index, source, parts=1, after=(), mib=16):
    shape = (index.shape[0] // parts,) + source.shape[1:]
    return call(
        gather_body, [(shape, source.dtype)] * parts, [index], [source], after=after, mib=mib
    )


def three(own_ref, near_ref, far_ref, i):
    return own_ref[i].astype(f32) + near_ref[i].astype(f32) + far_ref[i].astype(f32)


def output_body(
    row_ref, send_ref, bias_ref, scale_ref, held_ref, own_ref, near_ref, far_ref, t0, t1, t23,
    out_ref, sums_ref, token_ref, made, by_scale, by_bias, sems,
):
    quarter = t0.shape[0]
    more = [
        pltpu.make_async_copy(t, token_ref.at[pl.ds(k * quarter, quarter)], sems.at[k])
        for k, t in enumerate((t0, t1, t23.at[pl.ds(quarter, quarter)], t23.at[pl.ds(0, quarter)]))
    ]
    for copy in more:
        copy.start()
    scale = scale_ref[...]
    bias = bias_ref[...]
    wait(more)
    for i in range(held_ref.shape[0]):
        projected = three(own_ref, near_ref, far_ref, i) + bias
        tokens = token_ref[row_ref[i]].astype(f32)
        made[i] = (tokens + scale * projected).astype(bf16)
        d_output = held_ref[i].astype(f32)
        if i == 0:
            by_scale[...] = d_output * projected
            by_bias[...] = d_output * scale
        else:
            by_scale[...] += d_output * projected
            by_bias[...] += d_output * scale
    sums_ref[0:1] = jnp.sum(by_scale[...], axis=0, keepdims=True)
    sums_ref[1:2] = jnp.sum(by_bias[...], axis=0, keepdims=True)
    for i in range(out_ref.shape[0]):
        out_ref[i] = made[send_ref[i]]


def make_output(rows, sends, tokens, held, own, near, far, bias, scale, after):
    count, _, width = held.shape
    return call(
        output_body,
        [((sends.shape[0], BLOCK, width), bf16), ((2, width), f32)],
        [rows, sends],
        [bias, scale, held, own, near, far],
        scratch=[
            pltpu.VMEM((4 * count, BLOCK, width), bf16),
            pltpu.VMEM((count, BLOCK, width), bf16),
            pltpu.VMEM((BLOCK, width), f32),
            pltpu.VMEM((BLOCK, width), f32),
            pltpu.SemaphoreType.DMA((4,)),
        ],
        after=after,
        placed=tokens,
        mib=20,
    )


def d_tokens_body(
    row_ref, place_ref, gain_ref, token_ref, own_ref, near_ref, far_ref, d0, d1, d23,
    out_ref, held, sems,
):
    gain = gain_ref[...]
    quarter = held.shape[0] // 4
    mine = place_ref[3] * quarter
    more = [
        pltpu.make_async_copy(
            d.at[pl.ds(at + mine, quarter)], held.at[pl.ds(k * quarter, quarter)], sems.at[k]
        )
        for k, (d, at) in enumerate(((d0, 0), (d1, 0), (d23, 4 * quarter), (d23, 0)))
    ]
    for copy in more:
        copy.start()
    wait(more)
    for i in range(token_ref.shape[0]):
        tokens = token_ref[i].astype(f32)
        inverse = lax.rsqrt(jnp.mean(tokens * tokens, axis=-1, keepdims=True) + EPSILON)
        scaled = three(own_ref, near_ref, far_ref, i) * gain
        inner = jnp.mean(scaled * tokens, axis=-1, keepdims=True)
        d_output = held[row_ref[i]].astype(f32)
        out_ref[i] = (
            d_output + inverse * scaled - tokens * (inverse * inverse * inverse * inner)
        ).astype(bf16)


def make_d_tokens(rows, chip, tokens, d_parts, own, near, far, gain, after):
    return call(
        d_tokens_body,
        [(tokens.shape, bf16)],
        [rows, chip],
        [gain, tokens, own, near, far],
        scratch=[pltpu.VMEM(tokens.shape, bf16), pltpu.SemaphoreType.DMA((4,))],
        placed=d_parts,
        after=after,
        mib=12,
    )


def norm_rows(token_ref, first, count, gain, normed_ref, inverse_ref, start):
    rows = 32

    def some(k, _):
        at = pl.ds(pl.multiple_of(first + k * rows, rows), rows)
        tokens = token_ref[at, :].astype(f32)
        inverse = lax.rsqrt(jnp.mean(tokens * tokens, axis=-1, keepdims=True) + EPSILON)
        to = pl.ds(pl.multiple_of(start + k * rows, rows), rows)
        inverse_ref[to, :] = inverse
        normed_ref[to, :] = (tokens * inverse * gain).astype(bf16)
        return 0

    lax.fori_loop(0, count // rows, some, 0)


def softmax_of(query, keys, factor):
    scores = (
        lax.dot_general(query, keys, (((1,), (1,)), ((), ())), preferred_element_type=f32) * factor
    )
    top = jnp.max(scores, axis=-1, keepdims=True)
    weights = jnp.exp(scores - top)
    return weights / jnp.sum(weights, axis=-1, keepdims=True)


def permutation(place_ref, rows):
    columns = lax.broadcasted_iota(jnp.int32, (rows, rows), 1)
    return (place_ref[...] == columns).astype(f32).astype(bf16)


def ring_place(place_ref, axis, k):
    core = place_ref[0]
    return place_ref[axis] ^ (0, 1 + 2 * core, 2, 3 - 2 * core)[k]


def forward_body(
    copies, chip_ref, gain_ref, t0, t1, t23, w_ref, normed_ref, inverse_ref, qkv_ref
):
    rows = normed_ref.shape[0]
    part = rows // 4

    gain = gain_ref[...]
    for k, (tokens, at) in enumerate(((t0, 0), (t1, 0), (t23, part), (t23, 0))):
        start = pl.multiple_of(ring_place(chip_ref, 3, k) * part, part)
        norm_rows(tokens, at, part, gain, normed_ref, inverse_ref, start)
    for n in range(qkv_ref.shape[1] // 256):
        span = slice(n * 256, (n + 1) * 256)
        if n % 2 == 0:
            copies[0][n // 2].wait()
        qkv_ref[:, span] = jnp.dot(
            normed_ref[...], w_ref[:, span], preferred_element_type=f32
        ).astype(bf16)


def attend_body(factor, place_ref, qkv_ref, attended_ref, held):
    rows = qkv_ref.shape[0]
    for h in range(qkv_ref.shape[1] // (3 * HEAD_DIM)):
        for t in range(rows // TILE):
            span = slice(t * TILE, (t + 1) * TILE)
            at = 3 * h * HEAD_DIM
            query = qkv_ref[span, at : at + HEAD_DIM]
            keys = qkv_ref[span, at + HEAD_DIM : at + 2 * HEAD_DIM]
            values = qkv_ref[span, at + 2 * HEAD_DIM : at + 3 * HEAD_DIM]
            probs = softmax_of(query, keys, factor).astype(bf16)
            held[span, h * HEAD_DIM : (h + 1) * HEAD_DIM] = jnp.dot(
                probs, values, preferred_element_type=f32
            ).astype(bf16)
    perm = permutation(place_ref, rows)
    attended_ref[...] = lax.dot_general(
        perm, held[...], (((0,), (0,)), ((), ())), preferred_element_type=f32
    ).astype(bf16)


def forward(chip, tokens, gain, w_qkv, after):
    width, columns = w_qkv.shape
    rows = 4 * tokens[0].shape[0]
    return call(
        forward_body,
        [((rows, width), bf16), ((rows, 1), f32), ((rows, columns), bf16)],
        index=[chip],
        local=[gain, *tokens],
        fetched=[(w_qkv, 1, 3)],
        after=after,
        mib=FORWARD,
    )


def attend(qkv, place, after):
    rows, columns = qkv.shape
    return call(
        functools.partial(attend_body, HEAD_DIM**-0.5),
        [((rows, columns // 3), bf16)],
        local=[place, qkv],
        scratch=[pltpu.VMEM((rows, columns // 3), bf16)],
        after=after,
        mib=16,
    )


def split_rows(value, out_refs, span):
    at = 0
    for out_ref in out_refs:
        out_ref[:, span] = value[at : at + out_ref.shape[0]].astype(out_ref.dtype)
        at += out_ref.shape[0]


QUARTERS = (1, 2, 1)
STEP = 640


def head_body(copies, attended_ref, w_ref, *out_refs):
    for n, at in enumerate(range(0, w_ref.shape[1], STEP)):
        span = slice(at, at + STEP)
        copies[0][n].wait()
        full = jnp.dot(attended_ref[...], w_ref[:, span], preferred_element_type=f32)
        split_rows(full, out_refs, span)


def project(attended, w_out, after):
    rows, depth = attended.shape
    width = w_out.shape[1]
    return call(
        head_body,
        [((rows // 4 * n, width), bf16) for n in QUARTERS],
        local=[attended],
        fetched=[(w_out, 1, width // STEP)],
        after=after,
        mib=12,
    )


def back_body(
    factor, copies, scale_ref, qkv_ref, place_ref, d0, d1, d23, w_ref, scaled_ref, out_ref, held
):
    rows = qkv_ref.shape[0]
    part = rows // 4
    for k, (ref, at) in enumerate(((d0, 0), (d1, 0), (d23, part), (d23, 0))):
        term = ref[at : at + part].astype(f32) * scale_ref[...]
        scaled_ref[k * part : (k + 1) * part] = term.astype(bf16)
    wait(copies[0])
    total = lax.dot_general(
        scaled_ref[...], w_ref[...], (((1,), (1,)), ((), ())), preferred_element_type=f32
    ).astype(bf16)
    perm = permutation(place_ref, rows)
    held[...] = jnp.dot(perm, total, preferred_element_type=f32).astype(bf16)
    for h in range(qkv_ref.shape[1] // (3 * HEAD_DIM)):
        for t in range(rows // TILE):
            span = slice(t * TILE, (t + 1) * TILE)
            at = 3 * h * HEAD_DIM
            query = qkv_ref[span, at : at + HEAD_DIM]
            keys = qkv_ref[span, at + HEAD_DIM : at + 2 * HEAD_DIM]
            values = qkv_ref[span, at + 2 * HEAD_DIM : at + 3 * HEAD_DIM]
            d_att = held[span, h * HEAD_DIM : (h + 1) * HEAD_DIM]
            probs = softmax_of(query, keys, factor)
            d_probs = lax.dot_general(
                d_att, values, (((1,), (1,)), ((), ())), preferred_element_type=f32
            )
            d_values = lax.dot_general(
                probs.astype(bf16), d_att, (((0,), (0,)), ((), ())), preferred_element_type=f32
            )
            inner = jnp.sum(probs * d_probs, axis=-1, keepdims=True)
            d_scores = (probs * (d_probs - inner) * factor).astype(bf16)
            d_query = jnp.dot(d_scores, keys, preferred_element_type=f32)
            d_keys = lax.dot_general(
                d_scores, query, (((0,), (0,)), ((), ())), preferred_element_type=f32
            )
            out_ref[span, at : at + HEAD_DIM] = d_query.astype(bf16)
            out_ref[span, at + HEAD_DIM : at + 2 * HEAD_DIM] = d_keys.astype(bf16)
            out_ref[span, at + 2 * HEAD_DIM : at + 3 * HEAD_DIM] = d_values.astype(bf16)


def backward(parts, scale, w_out, qkv, place, after):
    depth, width = w_out.shape
    rows, columns = qkv.shape
    return call(
        functools.partial(back_body, HEAD_DIM**-0.5),
        [((rows, width), bf16), ((rows, columns), bf16)],
        local=[scale, qkv, place, *parts],
        fetched=[w_out],
        scratch=[pltpu.VMEM((rows, depth), bf16)],
        after=after,
        mib=20,
    )


def d_normed_body(
    copies, chip_ref, d_ref, inverse_ref, t0, t1, t23, w_ref, gain_ref, *refs
):
    out_refs, turned = refs[:3], refs[3]
    rows = t0.shape[0]
    inverses = []
    for k in range(4):
        at = pl.ds(pl.multiple_of(ring_place(chip_ref, 3, k) * rows, rows), rows)
        turned[k * rows : (k + 1) * rows] = d_ref[at, :]
        inverses.append(inverse_ref[at, :])
    for n, start in enumerate(range(0, w_ref.shape[0], STEP)):
        span = slice(start, start + STEP)
        copies[3][n].wait()
        full = lax.dot_general(
            turned[...], w_ref[span, :], (((1,), (1,)), ((), ())), preferred_element_type=f32
        )
        split_rows(full, out_refs, span)
        if n == 0:
            for each in copies[:3]:
                wait(each)
        total = jnp.zeros((1, STEP), f32)
        for k, (ref, at) in enumerate(((t0, 0), (t1, 0), (t23, rows), (t23, 0))):
            tokens = ref[at : at + rows, span].astype(f32)
            term = full[k * rows : (k + 1) * rows] * (tokens * inverses[k])
            total += jnp.sum(term, axis=0, keepdims=True)
        gain_ref[:, span] = total


def d_normed_parts(chip, d_qkv, w_qkv, tokens, inverse, after):
    rows, depth = d_qkv.shape
    width = w_qkv.shape[0]
    out = call(
        d_normed_body,
        [((1, width), f32)] + [((rows // 4 * n, width), bf16) for n in QUARTERS],
        [chip],
        [d_qkv, inverse],
        [*tokens, (w_qkv, 0, width // STEP)],
        [pltpu.VMEM(d_qkv.shape, bf16)],
        after,
        mib=26,
    )
    return out[0], out[1:]


def columns_of(ref, block):
    return ref[:, pl.ds(pl.multiple_of(block * 256, 256), 256)]


def products(left_a, right_a, left_b, right_b, store):
    turned = (((0,), (0,)), ((), ()))
    for at in range(0, left_a.shape[1], STEP):
        span = slice(at, at + STEP)
        store(
            span,
            lax.dot_general(left_a[:, span], right_a, turned, preferred_element_type=f32),
            lax.dot_general(left_b[:, span], right_b, turned, preferred_element_type=f32),
        )


def rights(place_ref, by_x, away, refs):
    half = 1 - place_ref[0] if away else place_ref[0]
    if by_x:
        normed, d_qkv = refs
        return normed, columns_of(d_qkv, 3 * half), normed, columns_of(d_qkv, 3 * half + 1)
    normed, d_qkv, scaled, attended = refs
    return normed, columns_of(d_qkv, 3 * half + 2), scaled, columns_of(attended, half)


def away_body(by_x, place_ref, *refs):
    out_ref = refs[-1]

    def store(span, first, second):
        out_ref[span, :256] = first.astype(bf16)
        out_ref[span, 256:] = second.astype(bf16)

    products(*rights(place_ref, by_x, True, refs[:-1]), store)


def here_body(by_x, place_ref, *refs):
    out_refs, total = refs[-4:-1], refs[-1]
    come_ref = refs[-5]

    def store(span, first, second):
        total[span, :256] = first + come_ref[span, :256].astype(f32)
        total[span, 256:] = second + come_ref[span, 256:].astype(f32)

    products(*rights(place_ref, by_x, False, refs[:-5]), store)
    chip_rows = total.shape[0] // 16
    for k in (1, 2, 3, 0):
        for i in range(4):
            ring = ring_place(place_ref, 1 if by_x else 2, k)
            at = (4 * ring + i if by_x else 4 * i + ring) * chip_rows
            part = total[pl.ds(pl.multiple_of(at, 8), chip_rows), :].astype(bf16)
            out_refs[(0, 1, 1, 2)[k]][4 * (k == 2) + i] = part


def column_products(place, by_x, operands, come=None, after=()):
    depth, width = operands[0].shape
    if come is None:
        return call(
            functools.partial(away_body, by_x),
            [((width, 512), bf16)],
            [place],
            operands,
            after=after,
            mib=16,
        )
    return call(
        functools.partial(here_body, by_x),
        [((4 * n, width // 16, 512), bf16) for n in QUARTERS],
        [place],
        [*operands, come],
        scratch=[pltpu.VMEM((width, 512), f32)],
        after=after,
        mib=26,
    )


def mid_body(along, place_ref, own_ref, near_ref, far_ref, *refs):
    out_refs, total = refs[:3], refs[3]
    for i in range(own_ref.shape[0]):
        total[i] = three(own_ref, near_ref, far_ref, i)
    for k in range(4):
        part = total[ring_place(place_ref, along, k)].astype(bf16)
        out_refs[(0, 1, 1, 2)[k]][1 if k == 2 else 0] = part


def regroup(along, place, own, near, far, after):
    return call(
        functools.partial(mid_body, along),
        [((n,) + own.shape[1:], bf16) for n in QUARTERS],
        [place],
        [own, near, far],
        scratch=[pltpu.VMEM(own.shape, f32)],
        after=after,
        mib=12,
    )


def last_body(place_ref, *refs):
    here_ref, there_ref = refs[6:]
    rows = here_ref.shape[0]
    for side in range(2):
        span = slice(512 * side, 512 * side + 512)
        total = three(*refs[3 * side : 3 * side + 3], 0)
        first = place_ref[0] == 0
        here_ref[:, span] = jnp.where(first, total[:rows], total[rows:]).astype(bf16)
        there_ref[:, span] = jnp.where(first, total[rows:], total[:rows]).astype(bf16)


def last_sums(place, left, right, after):
    shape = ((left[0].shape[1] // 2, 1024), bf16)
    return call(last_body, [shape, shape], [place], [*left, *right], after=after, mib=12)


def join_body(place_ref, here_ref, there_ref, qkv_ref, out_ref):
    first = place_ref[0] == 0
    here, there = here_ref[...].astype(f32), there_ref[...].astype(f32)
    low = jnp.where(first, here, there)
    high = jnp.where(first, there, here)
    qkv_ref[:, :768] = low[:, :768].astype(bf16)
    qkv_ref[:, 768:] = high[:, :768].astype(bf16)
    out_ref[:256] = low[:, 768:].T.astype(bf16)
    out_ref[256:] = high[:, 768:].T.astype(bf16)


def join(place, here, there, after):
    rows = here.shape[0]
    return call(
        join_body, [((rows, 1536), bf16), ((512, rows), bf16)], [place], [here, there], after=after, mib=12
    )


def swap_vision(x, flip):
    return lax.ppermute(x, "vision", [(i, i ^ flip) for i in range(4)])


def swap_dp(x, flip):
    return lax.ppermute(x, "dp", [(i, i ^ flip) for i in range(32)])


def pass_on(x, ring, second):
    pairs = []
    for i in range(128):
        at = {"x": i // 32, "y": i // 8 % 4, "core": i // 4 % 2, "vision": i % 4}
        at[ring] ^= 3 if (at["core"] == 0) == second else 1
        pairs.append((i, at["x"] * 32 + at["y"] * 8 + at["core"] * 4 + at["vision"]))
    return lax.ppermute(x, ("dp", "vision"), pairs)


def add_body(a_ref, b_ref, out_ref):
    out_ref[...] = (a_ref[...].astype(f32) + b_ref[...].astype(f32)).astype(out_ref.dtype)


def add(a, b, after, mib=8):
    return call(add_body, [(a.shape, a.dtype)], local=[a, b], after=after, mib=mib)


def hold_body(x_ref, out_ref):
    out_ref[...] = x_ref[...]


def hold(x, after):
    return call(hold_body, [(x.shape, x.dtype)], local=[x], after=after, mib=8)


def pair_body(a_ref, b_ref, out_ref):
    rows = a_ref.shape[0]
    out_ref[:rows] = a_ref[...]
    out_ref[rows:] = b_ref[...]


def pair(a, b, after):
    shape = (2 * a.shape[0],) + a.shape[1:]
    return call(pair_body, [(shape, a.dtype)], local=[a, b], after=after, mib=8)


def add_far_body(far_ref, near_ref, out_ref):
    rows = far_ref.shape[0]
    out_ref[...] = (far_ref[...].astype(f32) + near_ref[rows:].astype(f32)).astype(out_ref.dtype)


def add_far(far, near, after):
    return call(add_far_body, [(far.shape, far.dtype)], local=[far, near], after=after, mib=12)


def tables(dest, replica_rank, vision_rank):
    everyone = dest.reshape(32, 64)
    me = replica_rank * 4 + vision_rank
    row = lax.dynamic_index_in_dim(everyone, replica_rank, 0, keepdims=False)
    owner_vision = row // 16 % 4
    owner_replica = row // 64
    j = jnp.arange(64, dtype=jnp.int32)
    source = j // 16
    same = (
        (owner_vision[:, None] == owner_vision[None])
        & (source[:, None] == source[None])
        & (j[None] < j[:, None])
    )
    rank = jnp.sum(same.astype(jnp.int32), axis=1)
    way = jnp.where(replica_rank % 2 == 0, 1, 3)

    def steps(vision):
        return (way * (vision ^ vision_rank)) % 4

    arrival = steps(owner_vision) * 16 + source * 4 + rank

    def table(at, values, count):
        hit = at[None] == jnp.arange(count, dtype=jnp.int32)[:, None]
        return jnp.sum(jnp.where(hit, values[None], 0), axis=1)

    row_of_held = table(arrival, steps(source) * 16 + j % 16, 16)
    replica_of_held = table(arrival, owner_replica, 16)
    held_of_replica = table(replica_of_held, jnp.arange(16, dtype=jnp.int32), 32)
    slot_of_replica = jnp.sum(jnp.where(everyone // 16 == me, everyone % 16, 0), axis=1)
    hit = everyone[None] == (me * 16 + jnp.arange(16, dtype=jnp.int32))[:, None, None]
    replica_of_slot = jnp.sum(
        jnp.where(hit, jnp.arange(32, dtype=jnp.int32)[None, :, None], 0), axis=(1, 2)
    )
    own = lax.dynamic_slice_in_dim(arrival, vision_rank * 16, 16)
    return (
        arrival,
        row_of_held,
        replica_of_held,
        held_of_replica,
        slot_of_replica,
        replica_of_slot,
        own // 16 * 4 + own % 4,
    )


def body(tokens, gain, w_qkv, w_out, b_out, scale, dest, d_owned):
    vision_rank = lax.axis_index("vision")
    replica_rank = lax.axis_index("dp")
    rows_dev, width = tokens.shape
    x_rank, y_rank, core = replica_rank // 8, replica_rank // 2 % 4, replica_rank % 2
    chip = jnp.stack([core, x_rank, y_rank, vision_rank])

    def blocks(x):
        return x.reshape(-1, BLOCK, width)

    def row(x):
        return x.reshape(1, width)

    def to_dp(x):
        return lax.all_to_all(x, "dp", split_axis=0, concat_axis=0, tiled=True)

    (
        arrival,
        row_of_held,
        replica_of_held,
        held_of_replica,
        slot_of_replica,
        replica_of_slot,
        own_rows,
    ) = tables(dest, replica_rank, vision_rank)
    place = (arrival[:, None] * BLOCK + jnp.arange(BLOCK, dtype=jnp.int32)[None]).reshape(-1, 1)

    send_back = gather_blocks(slot_of_replica, blocks(d_owned))
    back = to_dp(send_back)
    near = pass_on(tokens, "vision", False)
    both = pair(tokens, near, [send_back])
    parts = [tokens, near, pass_on(both, "vision", True)]
    gain, scale, b_out = row(gain), row(scale), row(b_out)
    d_held = gather_blocks(replica_of_held, back, after=[both, place, gain])
    d_own = d_held.reshape(rows_dev, width)
    d_near = pass_on(d_own, "vision", False)

    normed, inverse, qkv = forward(chip, parts, gain, w_qkv, [d_held])
    both = pair(d_own, d_near, [qkv])
    attended = attend(qkv, place, [both])
    d_parts = [d_own, d_near, pass_on(both, "vision", True)]
    head = project(attended, w_out, [])
    first = hold(head[1], [d_parts[2]])
    head_near = pass_on(first, "vision", False)
    scaled, d_qkv = backward(d_parts, scale, w_out, qkv, place, [first])
    x_first = [normed, d_qkv]
    y_first = [normed, d_qkv, scaled, attended]
    left_away = column_products(chip, True, x_first)
    left_come = swap_dp(left_away, 1)
    right_away = column_products(chip, False, y_first, after=[left_away])
    right_come = swap_dp(right_away, 1)
    left = column_products(chip, True, x_first, left_come, [right_away])
    left_near = pass_on(left[1], "x", False)
    right = column_products(chip, False, y_first, right_come, [left[0]])
    right_near = pass_on(right[1], "y", False)
    total = add_far(head[2], head_near, [right[0]])
    head_far = pass_on(total, "vision", True)
    local_gain, pieces = d_normed_parts(chip, d_qkv, w_qkv, parts, inverse, [total])
    normed_near = pass_on(pieces[1], "vision", False)
    sends, scale_and_bias = make_output(
        row_of_held, held_of_replica, [blocks(p) for p in parts], d_held, blocks(head[0]),
        blocks(head_near), blocks(head_far), b_out, scale, [pieces[0]],
    )
    sums = jnp.concatenate([local_gain, scale_and_bias])
    sums_come = swap_dp(sums, 1)
    total = add_far(left[2], left_near, [sends])
    left_far = pass_on(total, "x", True)
    total = add_far(right[2], right_near, [total])
    right_far = pass_on(total, "y", True)
    sums = add(sums, sums_come, [total])
    sums_come = swap_vision(sums, 1)
    left = regroup(2, chip, left[0], left_near, left_far, [sums])
    left_near = pass_on(left[1], "y", False)
    sums = add(sums, sums_come, [left[0]])
    sums_come = swap_vision(sums, 3)
    right = regroup(1, chip, right[0], right_near, right_far, [sums])
    right_near = pass_on(right[1], "x", False)
    total = add_far(pieces[2], normed_near, [right[0]])
    normed_far = pass_on(total, "vision", True)
    sums = add(sums, sums_come, [total])
    sums_come = swap_dp(sums, 8)
    total = add_far(left[2], left_near, [sums])
    left_far = pass_on(total, "y", True)
    total = add_far(right[2], right_near, [total])
    right_far = pass_on(total, "x", True)
    sums = add(sums, sums_come, [total])
    sums_come = swap_dp(sums, 24)
    held = hold(sends, [sums])
    arrived = to_dp(held)
    d_tokens = make_d_tokens(
        own_rows, chip, blocks(tokens), [blocks(d) for d in d_parts], blocks(pieces[0]),
        blocks(normed_near), blocks(normed_far), gain, [held],
    ).reshape(rows_dev, width)
    here, there = last_sums(
        chip, [left[0], left_near, left_far], [right[0], right_near, right_far], [d_tokens]
    )
    there = swap_dp(there, 1)
    sums = add(sums, sums_come, [here])
    sums_come = swap_dp(sums, 2)
    y_owned = gather_blocks(replica_of_slot, arrived, after=[sums], mib=12)
    sums = add(sums, sums_come, [y_owned])
    sums_come = swap_dp(sums, 6)
    y_owned = y_owned.reshape(rows_dev, width)
    d_wqkv, d_wout = join(chip, here, there, [sums])
    sums = add(sums, sums_come, [d_wqkv])
    return y_owned, d_tokens, d_wqkv, d_wout, sums[0], sums[1], sums[2]


def solution(mesh):
    placed = (
        P(("dp", "vision"), None),
        P(),
        P(None, "vision"),
        P("vision", None),
        P(),
        P(),
        P(),
        P(("dp", "vision"), None),
    )
    return jax.shard_map(
        body,
        mesh=mesh,
        in_specs=placed,
        out_specs=(
            P(("dp", "vision"), None),
            P(("dp", "vision"), None),
            P("dp", "vision"),
            P("vision", "dp"),
            P(),
            P(),
            P(),
        ),
        check_vma=False,
    )
```
